128 devices in a mesh: beam: 8 (over z, x_hi), tm: 16 (over x_lo, y, core).
Axes of the slice: x: 4 (x_hi: 2, x_lo: 2; x = x_hi * 2 + x_lo), y: 4, z: 4, core: 2. Of those that a mesh axis runs over, the one named last changes fastest.
Arguments:
- spectra: bfloat16 [24, 2, 128, 64, 2048], P('beam', None, 'tm'), may hold values from -6 to 6
- prototype: float32 [12, 128], replicated, may hold values from -2 to 2
Outputs:
- voltages: bfloat16 [64, 24, 2, 262144], P('beam', None, None, 'tm')
The draws below stay inside these ranges and needn't reach their ends.
All inputs are finite; a program needn't handle non-finite values.
Results may differ from the reference program's by a relative error of at most 0.0058.
Values may be sent and summed in bfloat16 or wider, within the bound.
No kernel may reach another device: no remote copies, remote signals or barrier semaphores. Data moves between devices by JAX's collectives and lax.ppermute only.
A program may use at most 256 MiB of HBM per device.

```python
import math
import jax
import jax.numpy as jnp
from jax import lax

COARSE = 24
FINE = 128
TAPS = 12
BEAMS = 64
FRAMES = 2048


def levels(stream_key, shape, split, smallest, top_value):
    level, own = 1.0, jax.random.fold_in(stream_key, 6)
    for dim, blocks in split:
        heights = jnp.exp(jax.random.uniform(jax.random.fold_in(own, dim), (blocks,), jnp.float32, smallest / len(split), top_value / len(split)))
        level = level * jnp.repeat(heights, shape[dim] // blocks).reshape([-1 if axis == dim else 1 for axis in range(len(shape))])
    return level


def noise(key, extent, spread, limit, pieces=(), kind=jnp.bfloat16):
    gain = levels(key, extent, pieces, -0.22, 0.18) if pieces else 1.0
    result = jax.random.normal(key, extent, jnp.float32) * spread * gain
    return jnp.minimum(jnp.maximum(result, -limit), limit).astype(kind)


def setup_inputs(seed: int = 0) -> dict:
    seeds = jax.random.split(jax.random.key(seed), 3)
    spectra = noise(seeds[0], (COARSE, 2, FINE, BEAMS, FRAMES), 1.0, 6.0, ((0, 8), (2, 16)))
    prototype = noise(seeds[1], (TAPS, FINE), 0.3, 2.0, (), jnp.float32)
    return {"spectra": spectra, "prototype": prototype}


def synth_table(length):
    index = jnp.arange(length, dtype=jnp.int32)
    product = index[:, None] * index[None, :] % length
    angle = product.astype(jnp.float32) * jnp.float32(2.0 * math.pi / length)
    cosine = jnp.cos(angle) / jnp.float32(math.sqrt(length))
    sine = jnp.sin(angle) / jnp.float32(math.sqrt(length))
    real_row = jnp.stack([cosine, sine], axis=1)
    imag_row = jnp.stack([-sine, cosine], axis=1)
    return jnp.stack([real_row, imag_row], axis=0).astype(jnp.bfloat16)

def reference(spectra, prototype):
    table = synth_table(FINE).astype(jnp.float32)
    by_beam = jnp.moveaxis(spectra, 3, 0)
    edge = TAPS - 1

    def one_beam(block):
        frames = jnp.einsum('cpkf,pkqn->cqfn', block.astype(jnp.float32), table)
        frames = frames.astype(jnp.bfloat16)
        padded = jnp.concatenate([jnp.zeros((COARSE, 2, edge, FINE), jnp.bfloat16), frames], axis=2)
        filtered = jnp.zeros((COARSE, 2, FRAMES, FINE), jnp.float32)
        for tap_index in range(TAPS):
            filtered = filtered + prototype[tap_index] * padded[:, :, edge - tap_index:edge - tap_index + FRAMES, :].astype(jnp.float32)
        return filtered.reshape(COARSE, 2, FRAMES * FINE).astype(jnp.bfloat16)
    return lax.map(one_beam, by_beam)
```

```python
import functools
import math

import jax
import jax.numpy as jnp
from jax import lax
from jax.experimental import pallas as pl
from jax.experimental.pallas import tpu as pltpu
from jax.sharding import PartitionSpec as P

LATE, EARLY = 1, 0
UNITS = (
    ((0, LATE), (1, LATE), (2, LATE), (0, EARLY)),
    ((1, EARLY), (2, EARLY)),
)
LANES = 128
HALF = 64
HALO = 16
VMEM = 48 * 2**20


def pick(table, index):
    value = table[0]
    for place in range(1, len(table)):
        value = jnp.where(index == place, table[place], value)
    return value


def synth_table(length):
    index = jnp.arange(length, dtype=jnp.int32)
    product = index[:, None] * index[None, :] % length
    angle = product.astype(jnp.float32) * jnp.float32(2.0 * math.pi / length)
    cosine = jnp.cos(angle) / jnp.float32(math.sqrt(length))
    sine = jnp.sin(angle) / jnp.float32(math.sqrt(length))
    real_row = jnp.stack([cosine, sine], axis=1)
    imag_row = jnp.stack([-sine, cosine], axis=1)
    return jnp.stack([real_row, imag_row], axis=0).astype(jnp.bfloat16)


def pack_kernel(halves, blocks, x_ref, y_ref, rows_ref):
    half = pick(halves, pl.program_id(1))
    _, parts, fine, beams, _ = x_ref.shape
    group = beams // 2
    pair_rows = parts * fine
    lower = lax.broadcasted_iota(jnp.int32, (fine, LANES), 1) < HALF

    def one_block(t, carry):
        block = x_ref[0, :, :, :, pl.ds(pl.multiple_of(t * LANES, LANES), LANES)]
        rows_ref[...] = block.astype(jnp.float32).reshape(rows_ref.shape)

        def put(late):
            for g in range(2):
                for pair in range(group // 2):
                    made = []
                    for p in range(parts):
                        start = p * fine * beams + g * group + 2 * pair
                        even = rows_ref[pl.ds(start, fine, stride=beams), :]
                        odd = rows_ref[pl.ds(start + 1, fine, stride=beams), :]
                        if late:
                            made.append(jnp.where(lower, pltpu.roll(even, HALF, 1), odd))
                        else:
                            made.append(jnp.where(lower, even, pltpu.roll(odd, HALF, 1)))
                    packed = jnp.concatenate(made, axis=0).astype(jnp.bfloat16)
                    y_ref[g * blocks + t, 0, pl.ds(pair * pair_rows, pair_rows), :] = packed

        @pl.when(half == LATE)
        def _():
            put(True)

        @pl.when(half == EARLY)
        def _():
            put(False)

        return carry

    lax.fori_loop(0, blocks, one_block, 0)


def pack(spectra, units, groups, blocks):
    coarse, parts, fine, beams, frames = spectra.shape
    rows = (beams // groups) // 2 * parts * fine
    step_beams = 2 * (beams // groups)
    channels = tuple(c for c, _ in units)
    halves = tuple(h for _, h in units)
    return pl.pallas_call(
        functools.partial(pack_kernel, halves, blocks),
        grid=(groups // 2, len(units)),
        in_specs=[
            pl.BlockSpec(
                (1, parts, fine, step_beams, frames),
                lambda g, u: (pick(channels, u), 0, 0, g, 0),
            )
        ],
        out_specs=pl.BlockSpec((2 * blocks, 1, rows, LANES), lambda g, u: (g, u, 0, 0)),
        out_shape=jax.ShapeDtypeStruct((groups * blocks, len(units), rows, LANES), jnp.bfloat16),
        scratch_shapes=[pltpu.VMEM((parts * fine * step_beams, LANES), jnp.float32)],
        compiler_params=pltpu.CompilerParams(vmem_limit_bytes=VMEM),
        cost_estimate=pl.CostEstimate(
            flops=0, bytes_accessed=2 * 2 * groups * blocks * len(units) * rows * LANES, transcendentals=0
        ),
        name="pack",
    )(spectra)


def synth(block, table):
    rows = block.shape[0] * block.shape[1]
    return lax.dot_general(
        block.reshape(rows, LANES), table, (((0,), (0,)), ((), ())), preferred_element_type=jnp.float32
    )


def late_kernel(x_ref, table_ref, y_ref, lines_ref):
    table = table_ref[...]
    beams = y_ref.shape[1]
    pair_rows = x_ref.shape[3] // (beams // 2)
    for pair in range(beams // 2):
        made = synth(x_ref[0, :, 0, pair * pair_rows : (pair + 1) * pair_rows, :], table)
        for q in range(2):
            lines_ref[pair, pl.ds(q, LANES, stride=2), :] = made[:, q * LANES : (q + 1) * LANES]
        for one in range(2):
            y_ref[0, 2 * pair + one] = lines_ref[pair, one * 2 * HALF : (one + 1) * 2 * HALF, :].astype(jnp.bfloat16)


def late(received, table, units, beams):
    sources, blocks, count, rows, _ = received.shape
    places = [place for place, (_, h) in enumerate(units) if h == LATE]
    local = [units[place][0] for place in places]
    assert local == list(range(len(local)))
    n = len(places)
    return pl.pallas_call(
        late_kernel,
        grid=(sources, n),
        in_specs=[
            pl.BlockSpec((1, blocks, 1, rows, LANES), lambda s, i: (s, 0, pick(places, i), 0, 0)),
            pl.BlockSpec(table.shape, lambda s, i: (0, 0)),
        ],
        out_specs=pl.BlockSpec((1, beams, 2 * HALF, LANES), lambda s, i: (s * n + i, 0, 0, 0)),
        out_shape=jax.ShapeDtypeStruct((sources * n, beams, 2 * HALF, LANES), jnp.bfloat16),
        scratch_shapes=[pltpu.VMEM((beams // 2, 4 * HALF, LANES), jnp.float32)],
        compiler_params=pltpu.CompilerParams(vmem_limit_bytes=VMEM),
        cost_estimate=pl.CostEstimate(
            flops=2 * sources * n * (beams // 2) * LANES * 256 * 256,
            bytes_accessed=4 * sources * n * beams * 2 * HALF * LANES,
            transcendentals=0,
        ),
        name="synth_late",
    )(received, table)


def filter_kernel(n_in, x_ref, late_ref, halo_ref, table_ref, taps_ref, *rest):
    out_ref, lines_ref = rest[-2:]
    table = table_ref[...]
    beams = out_ref.shape[0]
    tap_count = taps_ref.shape[0]
    pair_rows = x_ref.shape[3] // (beams // 2)
    head = 2 * HALO
    total = 4 * HALF
    coefficients = [jnp.broadcast_to(taps_ref[j : j + 1, :], (8, LANES)) for j in range(tap_count)]
    for pair in range(beams // 2):
        made = synth(x_ref[0, :, 0, pair * pair_rows : (pair + 1) * pair_rows, :], table)
        made = made.astype(jnp.bfloat16).astype(jnp.float32)
        for one in range(2):
            beam = 2 * pair + one
            lines_ref[beam, 0:head, :] = halo_ref[0, beam].astype(jnp.float32)
            for q in range(2):
                lines_ref[beam, pl.ds(head + q, HALF, stride=2), :] = made[
                    one * HALF : (one + 1) * HALF, q * LANES : (q + 1) * LANES
                ]
            lines_ref[beam, head + 2 * HALF : head + total, :] = late_ref[0, beam].astype(jnp.float32)
            window = {}
            done = []
            for m in range(total // 8):
                acc = None
                for j in range(tap_count):
                    back, shift = j // 4, j % 4
                    key = (m - back, shift)
                    if key not in window:
                        start = head + 8 * (m - back) - 2 * shift
                        window[key] = lines_ref[beam, start : start + 8, :]
                    term = coefficients[j] * window[key]
                    acc = term if acc is None else acc + term
                done.append(acc)
                if len(done) == 2:
                    out_ref[beam, 0, 8 * (m - 1) : 8 * (m + 1), :] = jnp.concatenate(done, axis=0).astype(jnp.bfloat16)
                    done = []


def filtered(received, late_lines, halo, table, taps, units, coarse, beams, out):
    sources, blocks, _, rows, _ = received.shape
    places = [place for place, (_, h) in enumerate(units) if h == EARLY]
    local = [units[place][0] for place in places]
    n = len(places)
    total = 4 * HALF
    channel = lambda s, i: s * coarse + pick(local, i)
    in_specs = [
        pl.BlockSpec((1, blocks, 1, rows, LANES), lambda s, i: (s, 0, pick(places, i), 0, 0)),
        pl.BlockSpec((1, beams, 2 * HALF, LANES), lambda s, i: (channel(s, i), 0, 0, 0)),
        pl.BlockSpec((1, beams, 2 * HALO, LANES), lambda s, i: (channel(s, i), 0, 0, 0)),
        pl.BlockSpec(table.shape, lambda s, i: (0, 0)),
        pl.BlockSpec(taps.shape, lambda s, i: (0, 0)),
    ]
    operands = [received, late_lines, halo, table, taps]
    aliases = {}
    if out is not None:
        in_specs.append(pl.BlockSpec(memory_space=pl.ANY))
        operands.append(out)
        aliases = {len(operands) - 1: 0}
    return pl.pallas_call(
        functools.partial(filter_kernel, len(operands)),
        grid=(sources, n),
        in_specs=in_specs,
        out_specs=pl.BlockSpec((beams, 1, total, LANES), lambda s, i: (0, channel(s, i), 0, 0)),
        out_shape=jax.ShapeDtypeStruct((beams, sources * coarse, total, LANES), jnp.bfloat16),
        scratch_shapes=[pltpu.VMEM((beams, 2 * HALO + total, LANES), jnp.float32)],
        input_output_aliases=aliases,
        compiler_params=pltpu.CompilerParams(vmem_limit_bytes=VMEM),
        cost_estimate=pl.CostEstimate(
            flops=2 * sources * n * beams * total * LANES * (128 + 120),
            bytes_accessed=4 * sources * n * beams * total * LANES,
            transcendentals=0,
        ),
        name="filter",
    )(*operands)


def on_device(spectra, prototype):
    groups, blocks = lax.axis_size("beam"), lax.axis_size("tm")
    coarse, parts, fine, all_beams, _ = spectra.shape
    beams = all_beams // groups
    length = blocks * fine
    table = synth_table(length).reshape(parts, blocks, fine, 2 * length)
    table = table.transpose(1, 0, 2, 3).reshape(parts * length, 2 * length)
    received = []
    for units in UNITS:
        packed = pack(spectra, units, groups, blocks)
        moved = lax.all_to_all(packed, ("beam", "tm"), 0, 0, tiled=True)
        received.append(moved.reshape(groups, blocks, *moved.shape[1:]))
    late_lines = late(received[0], table, UNITS[0], beams)
    route = [(i, i + 1) for i in range(blocks - 1)]
    halo = lax.ppermute(late_lines[:, :, 2 * (HALF - HALO) :, :], "tm", route)
    out = None
    for units, moved in zip(UNITS, received):
        if any(h == EARLY for _, h in units):
            out = filtered(moved, late_lines, halo, table, prototype, units, coarse, beams, out)
    channels = groups * coarse
    out = out.reshape(beams, channels, 2 * HALF, 2, LANES).swapaxes(2, 3)
    return out.reshape(beams, channels, 2, 2 * HALF * LANES)


def solution(mesh):
    in_specs = (P("beam", None, "tm", None, None), P())
    out_specs = P("beam", None, None, "tm")
    return jax.shard_map(on_device, mesh=mesh, in_specs=in_specs, out_specs=out_specs, check_vma=False)
```

```python
import functools
import math

import jax
import jax.numpy as jnp
from jax import lax
from jax.experimental import pallas as pl
from jax.experimental.pallas import tpu as pltpu
from jax.sharding import PartitionSpec as P

EARLY, LATE = 0, 1
UNITS = (
    ((0, LATE), (1, LATE), (2, LATE), (0, EARLY)),
    ((1, EARLY), (2, EARLY)),
)
LANES = 128
HALF = 64
EDGE = 16
HALO = 11
ROWS = 4 * HALF
SPLIT = 2 * (HALF + EDGE)
VMEM = 40 * 2**20


def synth_table(length):
    index = jnp.arange(length, dtype=jnp.int32)
    product = index[:, None] * index[None, :] % length
    angle = product.astype(jnp.float32) * jnp.float32(2.0 * math.pi / length)
    cosine = jnp.cos(angle) / jnp.float32(math.sqrt(length))
    sine = jnp.sin(angle) / jnp.float32(math.sqrt(length))
    real_row = jnp.stack([cosine, sine], axis=1)
    imag_row = jnp.stack([-sine, cosine], axis=1)
    return jnp.stack([real_row, imag_row], axis=0).astype(jnp.bfloat16)


def row_order(parts, fine, beams):
    count = 2 * parts * fine * (beams // 2)
    row = lax.broadcasted_iota(jnp.int32, (count, count), 0)
    column = lax.broadcasted_iota(jnp.int32, (count, count), 1)
    within = row % (parts * fine)
    pairs = beams // 4
    pair = row // (parts * fine) % pairs
    parity = row // (parts * fine * pairs) % 2
    group = row // (parts * fine * pairs * 2)
    return (column == within * beams + group * 2 * pairs + 2 * pair + parity).astype(jnp.bfloat16)


def pack_kernel(units, blocks, x_ref, order_ref, y_ref, x_buf, y_buf, x_sem, y_sem):
    channels = sorted({c for c, _ in units})
    _, parts, fine, all_beams, frames = x_ref.shape
    beams = 16
    strips = all_beams // beams
    rows = y_ref.shape[2]

    def load(i, g):
        where = (slice(None), slice(None), pl.ds(pl.multiple_of(g * beams, beams), beams), slice(None))
        return pltpu.make_async_copy(x_ref.at[(channels[i], *where)], x_buf.at[(i, *where)], x_sem.at[i, g])

    def store(u, g):
        where = (pl.ds(g * 2 * blocks, 2 * blocks), u)
        return pltpu.make_async_copy(y_buf.at[where], y_ref.at[where], y_sem.at[u, g])

    for i in range(len(channels)):
        for g in range(strips):
            load(i, g).start()
    order = order_ref[...]
    lower = lax.broadcasted_iota(jnp.int32, (rows, LANES), 1) < HALF

    for i, channel in enumerate(channels):
        own = [(u, h) for u, (c, h) in enumerate(units) if c == channel]

        def strip(g, carry):
            load(i, g).wait()
            for t in range(0, blocks, 2):
                lines = x_buf[i, :, :, pl.ds(pl.multiple_of(g * beams, beams), beams), t * LANES : (t + 2) * LANES]
                lines = lines.reshape(parts * fine * beams, 2 * LANES)
                moved = jnp.dot(order, lines, preferred_element_type=jnp.float32)
                for part in range(2):
                    for group in range(2):
                        block = moved[2 * group * rows : 2 * (group + 1) * rows, part * LANES : (part + 1) * LANES]
                        even, odd = block[:rows], block[rows:]
                        for u, h in own:
                            if h == LATE:
                                made = jnp.where(lower, pltpu.roll(even, HALF, 1), odd)
                            else:
                                made = jnp.where(lower, even, pltpu.roll(odd, HALF, 1))
                            y_buf[(2 * g + group) * blocks + t + part, u] = made.astype(jnp.bfloat16)
            for u, _ in own:
                store(u, g).start()
            return carry

        lax.fori_loop(0, strips, strip, 0)
    for u in range(len(units)):
        for g in range(strips):
            store(u, g).wait()


def pack(spectra, units, groups, blocks):
    coarse, parts, fine, beams, frames = spectra.shape
    rows = (beams // groups) // 2 * parts * fine
    strips = beams // 16
    channels = len({c for c, _ in units})
    order = row_order(parts, fine, 16)
    shape = (groups * blocks, len(units), rows, LANES)
    return pl.pallas_call(
        functools.partial(pack_kernel, units, blocks),
        in_specs=[pl.BlockSpec(memory_space=pl.ANY), pl.BlockSpec(memory_space=pltpu.VMEM)],
        out_specs=pl.BlockSpec(memory_space=pl.ANY),
        out_shape=jax.ShapeDtypeStruct(shape, jnp.bfloat16),
        scratch_shapes=[
            pltpu.VMEM((channels, parts, fine, beams, frames), jnp.bfloat16),
            pltpu.VMEM(shape, jnp.bfloat16),
            pltpu.SemaphoreType.DMA((channels, strips)),
            pltpu.SemaphoreType.DMA((len(units), strips)),
        ],
        compiler_params=pltpu.CompilerParams(vmem_limit_bytes=VMEM),
        cost_estimate=pl.CostEstimate(
            flops=channels * 2 * 256 * 256 * strips * frames,
            bytes_accessed=2 * channels * parts * fine * beams * frames + 2 * math.prod(shape),
            transcendentals=0,
        ),
        name="pack",
    )(spectra, order)


def synth(block, table):
    rows = block.shape[0] * block.shape[1]
    made = lax.dot_general(
        block.reshape(rows, LANES), table, (((0,), (0,)), ((), ())), preferred_element_type=jnp.float32
    )
    return made.astype(jnp.bfloat16).astype(jnp.float32)


def interleave(lines_ref, made, beam, one, start):
    for q in range(2):
        lines_ref[beam, pl.ds(start + q, HALF, stride=2), :] = made[
            one * HALF : (one + 1) * HALF, q * LANES : (q + 1) * LANES
        ]


def fir(lines_ref, beam, coefficients, start, count, out_ref, where):
    window = {}
    done = []
    for m in range(count // 8):
        total = None
        for j, coefficient in enumerate(coefficients):
            key = (m - j // 4, j % 4)
            if key not in window:
                first = start + 8 * key[0] - 2 * key[1]
                window[key] = lines_ref[beam, first : first + 8, :]
            term = coefficient * window[key]
            total = term if total is None else total + term
        done.append(total)
        if len(done) == 2:
            out_ref[(*where, pl.ds(8 * (m - 1), 16), slice(None))] = jnp.concatenate(done, axis=0).astype(jnp.bfloat16)
            done = []


def spread(taps_ref):
    return [jnp.broadcast_to(taps_ref[j : j + 1, :], (8, LANES)) for j in range(taps_ref.shape[0])]


def late_kernel(coarse, x_ref, table_ref, taps_ref, out_ref, edge_ref, halo_ref, *scratch):
    x_buf, out_buf, edge_buf, halo_buf, lines, tail, x_sem, out_sem, edge_sem, halo_sem = scratch
    beams = out_ref.shape[0]
    channels = out_ref.shape[1]
    pair_rows = x_ref.shape[3] // (beams // 2)

    def load(c):
        return pltpu.make_async_copy(x_ref.at[c // coarse, :, c % coarse], x_buf.at[c], x_sem.at[c])

    def stores(c):
        return (
            pltpu.make_async_copy(out_buf.at[c], out_ref.at[:, c, pl.ds(SPLIT, ROWS - SPLIT)], out_sem.at[c]),
            pltpu.make_async_copy(edge_buf.at[c], edge_ref.at[c], edge_sem.at[c]),
            pltpu.make_async_copy(halo_buf.at[c], halo_ref.at[c], halo_sem.at[c]),
        )

    for c in range(channels):
        load(c).start()
    table = table_ref[...]
    coefficients = spread(taps_ref)

    def channel(c, carry):
        load(c).wait()
        for pair in range(beams // 2):
            made = synth(x_buf[c, :, pair * pair_rows : (pair + 1) * pair_rows, :], table)
            for one in range(2):
                beam = 2 * pair + one
                interleave(lines, made, beam, one, 0)
                edge_buf[c, beam] = lines[beam, : 2 * EDGE, :].astype(jnp.bfloat16)
                tail[2 * HALO * beam : 2 * HALO * (beam + 1), :] = lines[beam, 2 * (HALF - HALO) : 2 * HALF, :]
                fir(lines, beam, coefficients, 2 * EDGE, ROWS - SPLIT, out_buf, (c, beam))
        halo_buf[c] = tail[...].astype(jnp.bfloat16)
        for copy in stores(c):
            copy.start()
        return carry

    lax.fori_loop(0, channels, channel, 0)
    for c in range(channels):
        for copy in stores(c):
            copy.wait()


def late(received, table, taps, coarse, beams):
    sources, blocks, _, rows, _ = received.shape
    channels = sources * coarse
    anywhere = pl.BlockSpec(memory_space=pl.ANY)
    inside = pl.BlockSpec(memory_space=pltpu.VMEM)
    edge = (channels, beams, 2 * EDGE, LANES)
    halo = (channels, beams * 2 * HALO, LANES)
    return pl.pallas_call(
        functools.partial(late_kernel, coarse),
        in_specs=[anywhere, inside, inside],
        out_specs=[anywhere, anywhere, anywhere],
        out_shape=[
            jax.ShapeDtypeStruct((beams, channels, ROWS, LANES), jnp.bfloat16),
            jax.ShapeDtypeStruct(edge, jnp.bfloat16),
            jax.ShapeDtypeStruct(halo, jnp.bfloat16),
        ],
        scratch_shapes=[
            pltpu.VMEM((channels, blocks, rows, LANES), jnp.bfloat16),
            pltpu.VMEM((channels, beams, ROWS - SPLIT, LANES), jnp.bfloat16),
            pltpu.VMEM(edge, jnp.bfloat16),
            pltpu.VMEM(halo, jnp.bfloat16),
            pltpu.VMEM((beams, 2 * HALF, LANES), jnp.float32),
            pltpu.VMEM((beams * 2 * HALO, LANES), jnp.float32),
            pltpu.SemaphoreType.DMA((channels,)),
            pltpu.SemaphoreType.DMA((channels,)),
            pltpu.SemaphoreType.DMA((channels,)),
            pltpu.SemaphoreType.DMA((channels,)),
        ],
        compiler_params=pltpu.CompilerParams(vmem_limit_bytes=VMEM),
        cost_estimate=pl.CostEstimate(
            flops=channels * beams * HALF * 2 * 256 * 256,
            bytes_accessed=2 * channels * beams * (4 * HALF + ROWS - SPLIT) * LANES,
            transcendentals=0,
        ),
        name="late",
    )(received, table, taps)


def filter_kernel(units, coarse, x_ref, edge_ref, halo_ref, table_ref, taps_ref, _, out_ref, *scratch):
    x_buf, edge_buf, halo_buf, out_buf, lines, tail, x_sem, edge_sem, halo_sem, out_sem = scratch
    beams = out_ref.shape[0]
    sources = x_ref.shape[0]
    pair_rows = x_ref.shape[3] // (beams // 2)
    head = 32
    places = [(place, c) for place, (c, h) in enumerate(units) if h == EARLY]
    n = len(places)
    assert all(b == (a[0] + 1, a[1] + 1) for a, b in zip(places, places[1:]))
    place, first = places[0]

    def loads(i):
        s, k = i // n, i % n
        c = s * coarse + first + k
        return (
            pltpu.make_async_copy(x_ref.at[s, :, place + k], x_buf.at[i], x_sem.at[i]),
            pltpu.make_async_copy(edge_ref.at[c], edge_buf.at[i], edge_sem.at[i]),
            pltpu.make_async_copy(halo_ref.at[c], halo_buf.at[i], halo_sem.at[i]),
        )

    def store(i):
        c = (i // n) * coarse + first + i % n
        return pltpu.make_async_copy(out_buf.at[i], out_ref.at[:, c, pl.ds(0, SPLIT)], out_sem.at[i])

    for i in range(sources * n):
        for copy in loads(i):
            copy.start()
    table = table_ref[...]
    coefficients = spread(taps_ref)

    def channel(i, carry):
        for copy in loads(i):
            copy.wait()
        tail[...] = halo_buf[i].astype(jnp.float32)
        for pair in range(beams // 2):
            made = synth(x_buf[i, :, pair * pair_rows : (pair + 1) * pair_rows, :], table)
            for one in range(2):
                beam = 2 * pair + one
                lines[beam, head - 2 * HALO : head, :] = tail[2 * HALO * beam : 2 * HALO * (beam + 1), :]
                interleave(lines, made, beam, one, head)
                lines[beam, head + 2 * HALF : head + SPLIT, :] = edge_buf[i, beam].astype(jnp.float32)
                fir(lines, beam, coefficients, head, SPLIT, out_buf, (i, beam))
        store(i).start()
        return carry

    lax.fori_loop(0, sources * n, channel, 0)
    for i in range(sources * n):
        store(i).wait()


def filtered(received, edge, halo, table, taps, out, units, coarse):
    sources, blocks, _, rows, _ = received.shape
    beams = out.shape[0]
    count = sources * sum(h == EARLY for _, h in units)
    anywhere = pl.BlockSpec(memory_space=pl.ANY)
    inside = pl.BlockSpec(memory_space=pltpu.VMEM)
    return pl.pallas_call(
        functools.partial(filter_kernel, units, coarse),
        in_specs=[anywhere, anywhere, anywhere, inside, inside, anywhere],
        out_specs=anywhere,
        out_shape=jax.ShapeDtypeStruct(out.shape, out.dtype),
        scratch_shapes=[
            pltpu.VMEM((count, blocks, rows, LANES), jnp.bfloat16),
            pltpu.VMEM((count, *edge.shape[1:]), jnp.bfloat16),
            pltpu.VMEM((count, *halo.shape[1:]), jnp.bfloat16),
            pltpu.VMEM((count, beams, SPLIT, LANES), jnp.bfloat16),
            pltpu.VMEM((beams, 32 + SPLIT, LANES), jnp.float32),
            pltpu.VMEM(halo.shape[1:], jnp.float32),
            pltpu.SemaphoreType.DMA((count,)),
            pltpu.SemaphoreType.DMA((count,)),
            pltpu.SemaphoreType.DMA((count,)),
            pltpu.SemaphoreType.DMA((count,)),
        ],
        input_output_aliases={5: 0},
        compiler_params=pltpu.CompilerParams(vmem_limit_bytes=VMEM),
        cost_estimate=pl.CostEstimate(
            flops=count * beams * HALF * 2 * 256 * 256,
            bytes_accessed=2 * count * beams * (2 * HALF + SPLIT + 64) * LANES,
            transcendentals=0,
        ),
        name="filter",
    )(received, edge, halo, table, taps, out)


def on_device(spectra, prototype):
    groups, blocks = lax.axis_size("beam"), lax.axis_size("tm")
    coarse, parts, fine, all_beams, _ = spectra.shape
    beams = all_beams // groups
    length = blocks * fine
    table = synth_table(length).reshape(parts, blocks, fine, 2 * length)
    table = table.transpose(1, 0, 2, 3).reshape(parts * length, 2 * length)
    received = []
    for units in UNITS:
        packed = pack(spectra, units, groups, blocks)
        moved = lax.all_to_all(packed, ("beam", "tm"), 0, 0, tiled=True)
        received.append(moved.reshape(groups, blocks, *moved.shape[1:]))
    out, edge, halo = late(received[0], table, prototype, coarse, beams)
    halo = lax.ppermute(halo, "tm", [(i, i + 1) for i in range(blocks - 1)])
    for units, moved in zip(UNITS, received):
        if any(h == EARLY for _, h in units):
            out = filtered(moved, edge, halo, table, prototype, out, units, coarse)
    channels = groups * coarse
    out = out.reshape(beams, channels, 2 * HALF, 2, LANES).swapaxes(2, 3)
    return out.reshape(beams, channels, 2, 2 * HALF * LANES)


def solution(mesh):
    in_specs = (P("beam", None, "tm", None, None), P())
    out_specs = P("beam", None, None, "tm")
    return jax.shard_map(on_device, mesh=mesh, in_specs=in_specs, out_specs=out_specs, check_vma=False)
```

```python
import functools
import math

import jax
import jax.numpy as jnp
from jax import lax
from jax.experimental import pallas as pl
from jax.experimental.pallas import tpu as pltpu
from jax.sharding import PartitionSpec as P

EARLY, LATE = 0, 1
UNITS = ((0, EARLY), (1, EARLY), (2, EARLY), (0, LATE), (1, LATE), (2, LATE))
LANES = 128
HALF = 64
EDGE = 16
HALO = 11
ROWS = 4 * HALF
SPLIT = 2 * (HALF + EDGE)
HEAD = 2 * EDGE
VMEM = 40 * 2**20


def synth_table(length):
    index = jnp.arange(length, dtype=jnp.int32)
    product = index[:, None] * index[None, :] % length
    angle = product.astype(jnp.float32) * jnp.float32(2.0 * math.pi / length)
    cosine = jnp.cos(angle) / jnp.float32(math.sqrt(length))
    sine = jnp.sin(angle) / jnp.float32(math.sqrt(length))
    real_row = jnp.stack([cosine, sine], axis=1)
    imag_row = jnp.stack([-sine, cosine], axis=1)
    return jnp.stack([real_row, imag_row], axis=0).astype(jnp.bfloat16)


def row_order(parts, fine, beams):
    count = 2 * parts * fine * (beams // 2)
    row = lax.broadcasted_iota(jnp.int32, (count, count), 0)
    column = lax.broadcasted_iota(jnp.int32, (count, count), 1)
    within = row % (parts * fine)
    pairs = beams // 4
    pair = row // (parts * fine) % pairs
    parity = row // (parts * fine * pairs) % 2
    group = row // (parts * fine * pairs * 2)
    return (column == within * beams + group * 2 * pairs + 2 * pair + parity).astype(jnp.bfloat16)


def pack_kernel(units, blocks, x_ref, order_ref, y_ref, x_buf, y_buf, x_sem, y_sem):
    channels = sorted({c for c, _ in units})
    _, parts, fine, all_beams, frames = x_ref.shape
    beams = 16
    strips = all_beams // beams
    rows = y_ref.shape[2]

    def load(i, g):
        where = (slice(None), slice(None), pl.ds(pl.multiple_of(g * beams, beams), beams), slice(None))
        return pltpu.make_async_copy(x_ref.at[(channels[i], *where)], x_buf.at[(i, *where)], x_sem.at[i, g])

    def store(u, g):
        where = (pl.ds(g * 2 * blocks, 2 * blocks), u)
        return pltpu.make_async_copy(y_buf.at[where], y_ref.at[where], y_sem.at[u, g])

    for i in range(len(channels)):
        for g in range(strips):
            load(i, g).start()
    order = order_ref[...]
    lower = lax.broadcasted_iota(jnp.int32, (rows, LANES), 1) < HALF

    for i, channel in enumerate(channels):
        own = [(u, h) for u, (c, h) in enumerate(units) if c == channel]

        def strip(g, carry):
            load(i, g).wait()
            for t in range(0, blocks, 2):
                lines = x_buf[i, :, :, pl.ds(pl.multiple_of(g * beams, beams), beams), t * LANES : (t + 2) * LANES]
                lines = lines.reshape(parts * fine * beams, 2 * LANES)
                moved = jnp.dot(order, lines, preferred_element_type=jnp.float32)
                for part in range(2):
                    for group in range(2):
                        block = moved[2 * group * rows : 2 * (group + 1) * rows, part * LANES : (part + 1) * LANES]
                        even, odd = block[:rows], pltpu.roll(block[rows:], HALF, 1)
                        for u, h in own:
                            made = jnp.where(lower, odd, even) if h == LATE else jnp.where(lower, even, odd)
                            y_buf[(2 * g + group) * blocks + t + part, u] = made.astype(jnp.bfloat16)
            for u, _ in own:
                store(u, g).start()
            return carry

        lax.fori_loop(0, strips, strip, 0)
    for u in range(len(units)):
        for g in range(strips):
            store(u, g).wait()


def pack(spectra, units, groups, blocks):
    coarse, parts, fine, beams, frames = spectra.shape
    rows = (beams // groups) // 2 * parts * fine
    strips = beams // 16
    channels = len({c for c, _ in units})
    order = row_order(parts, fine, 16)
    shape = (groups * blocks, len(units), rows, LANES)
    return pl.pallas_call(
        functools.partial(pack_kernel, units, blocks),
        in_specs=[pl.BlockSpec(memory_space=pl.ANY), pl.BlockSpec(memory_space=pltpu.VMEM)],
        out_specs=pl.BlockSpec(memory_space=pl.ANY),
        out_shape=jax.ShapeDtypeStruct(shape, jnp.bfloat16),
        scratch_shapes=[
            pltpu.VMEM((channels, parts, fine, beams, frames), jnp.bfloat16),
            pltpu.VMEM(shape, jnp.bfloat16),
            pltpu.SemaphoreType.DMA((channels, strips)),
            pltpu.SemaphoreType.DMA((len(units), strips)),
        ],
        compiler_params=pltpu.CompilerParams(vmem_limit_bytes=VMEM),
        cost_estimate=pl.CostEstimate(
            flops=channels * 2 * 256 * 256 * strips * frames,
            bytes_accessed=2 * channels * parts * fine * beams * frames + 2 * math.prod(shape),
            transcendentals=0,
        ),
        name="pack",
    )(spectra, order)


def synth(block, table):
    rows = block.shape[0] * block.shape[1]
    made = lax.dot_general(
        block.reshape(rows, LANES), table, (((0,), (0,)), ((), ())), preferred_element_type=jnp.float32
    )
    return made.astype(jnp.bfloat16).astype(jnp.float32)


def interleave(lines_ref, made, beam, one, start):
    for q in range(2):
        lines_ref[beam, pl.ds(start + q, HALF, stride=2), :] = made[
            one * HALF : (one + 1) * HALF, q * LANES : (q + 1) * LANES
        ]


def fir(lines_ref, beam, coefficients, start, count, out_ref, where):
    window = {}
    done = []
    for m in range(count // 8):
        total = None
        for j, coefficient in enumerate(coefficients):
            key = (m - j // 4, j % 4)
            if key not in window:
                first = start + 8 * key[0] - 2 * key[1]
                window[key] = lines_ref[beam, first : first + 8, :]
            term = coefficient * window[key]
            total = term if total is None else total + term
        done.append(total)
        if len(done) == 2:
            out_ref[(*where, pl.ds(8 * (m - 1), 16), slice(None))] = jnp.concatenate(done, axis=0).astype(jnp.bfloat16)
            done = []


def spread(taps_ref):
    return [jnp.broadcast_to(taps_ref[j : j + 1, :], (8, LANES)) for j in range(taps_ref.shape[0])]


def in_turn(count, pairs, wait, make, use, finish):
    wait(0)
    for pair in range(pairs):
        make(0, 0, pair)

    def two(step, carry):
        for slot in range(2):
            now = 2 * step + slot
            if slot == 0:
                wait(now + 1)
                later = now + 1
            else:
                later = jnp.minimum(now + 1, count - 1)

                @pl.when(now + 1 < count)
                def _():
                    wait(later)

            for pair in range(pairs):
                make(later, 1 - slot, pair)
                use(now, slot, pair)
            finish(now)
        return carry

    lax.fori_loop(0, count // 2, two, 0)


def grouped(count, size, loads, stores):
    for group in range(count // size):
        for copy in loads(group):
            copy.start()

    def wait(i):
        @pl.when(i % size == 0)
        def _():
            for copy in loads(i // size):
                copy.wait()

    def finish(i):
        @pl.when(i % size == size - 1)
        def _():
            for copy in stores(i // size):
                copy.start()

    def drain():
        for group in range(count // size):
            for copy in stores(group):
                copy.wait()

    return wait, finish, drain


def late_kernel(coarse, x_ref, table_ref, taps_ref, out_ref, edge_ref, halo_ref, *scratch):
    x_buf, out_buf, edge_buf, halo_buf, lines_a, lines_b, tail, x_sem, out_sem, edge_sem, halo_sem = scratch
    lines = (lines_a, lines_b)
    beams, channels = out_ref.shape[:2]
    pair_rows = x_ref.shape[3] // (beams // 2)
    table = table_ref[...]
    coefficients = spread(taps_ref)

    def loads(s):
        where = x_ref.at[s, :, pl.ds(LATE * coarse, coarse)]
        return (pltpu.make_async_copy(where, x_buf.at[s], x_sem.at[s]),)

    def stores(s):
        own = pl.ds(s * coarse, coarse)
        rows = pl.ds(SPLIT, ROWS - SPLIT)
        return (
            pltpu.make_async_copy(out_buf.at[:, own], out_ref.at[:, own, rows], out_sem.at[s]),
            pltpu.make_async_copy(edge_buf.at[own], edge_ref.at[own], edge_sem.at[s]),
            pltpu.make_async_copy(halo_buf.at[own], halo_ref.at[own], halo_sem.at[s]),
        )

    wait, send, drain = grouped(channels, coarse, loads, stores)

    def make(c, slot, pair):
        rows = slice(pair * pair_rows, (pair + 1) * pair_rows)
        made = synth(x_buf[c // coarse, :, c % coarse, rows, :], table)
        for one in range(2):
            interleave(lines[slot], made, 2 * pair + 1 - one, one, 0)

    def use(c, slot, pair):
        for beam in (2 * pair, 2 * pair + 1):
            edge_buf[c, beam] = lines[slot][beam, : 2 * EDGE, :].astype(jnp.bfloat16)
            tail[2 * HALO * beam : 2 * HALO * (beam + 1), :] = lines[slot][beam, 2 * (HALF - HALO) : 2 * HALF, :]
            fir(lines[slot], beam, coefficients, 2 * EDGE, ROWS - SPLIT, out_buf, (beam, c))

    def finish(c):
        halo_buf[c] = tail[...].astype(jnp.bfloat16)
        send(c)

    in_turn(channels, beams // 2, wait, make, use, finish)
    drain()


def late(received, table, taps, coarse, beams):
    sources, blocks, _, rows, _ = received.shape
    channels = sources * coarse
    anywhere = pl.BlockSpec(memory_space=pl.ANY)
    inside = pl.BlockSpec(memory_space=pltpu.VMEM)
    edge = (channels, beams, 2 * EDGE, LANES)
    halo = (channels, beams * 2 * HALO, LANES)
    return pl.pallas_call(
        functools.partial(late_kernel, coarse),
        in_specs=[anywhere, inside, inside],
        out_specs=[anywhere, anywhere, anywhere],
        out_shape=[
            jax.ShapeDtypeStruct((beams, channels, ROWS, LANES), jnp.bfloat16),
            jax.ShapeDtypeStruct(edge, jnp.bfloat16),
            jax.ShapeDtypeStruct(halo, jnp.bfloat16),
        ],
        scratch_shapes=[
            pltpu.VMEM((sources, blocks, coarse, rows, LANES), jnp.bfloat16),
            pltpu.VMEM((beams, channels, ROWS - SPLIT, LANES), jnp.bfloat16),
            pltpu.VMEM(edge, jnp.bfloat16),
            pltpu.VMEM(halo, jnp.bfloat16),
            pltpu.VMEM((beams, 2 * HALF, LANES), jnp.float32),
            pltpu.VMEM((beams, 2 * HALF, LANES), jnp.float32),
            pltpu.VMEM((beams * 2 * HALO, LANES), jnp.float32),
            pltpu.SemaphoreType.DMA((channels,)),
            pltpu.SemaphoreType.DMA((channels,)),
            pltpu.SemaphoreType.DMA((channels,)),
            pltpu.SemaphoreType.DMA((channels,)),
        ],
        compiler_params=pltpu.CompilerParams(vmem_limit_bytes=VMEM),
        cost_estimate=pl.CostEstimate(
            flops=channels * beams * HALF * 2 * 256 * 256,
            bytes_accessed=2 * channels * beams * (4 * HALF + ROWS - SPLIT) * LANES,
            transcendentals=0,
        ),
        name="late",
    )(received, table, taps)


def middle_kernel(coarse, x_ref, edge_ref, table_ref, taps_ref, _, out_ref, begin_ref, *scratch):
    x_buf, edge_buf, out_buf, begin_buf, lines_a, lines_b, x_sem, edge_sem, out_sem, begin_sem = scratch
    lines = (lines_a, lines_b)
    beams, channels = out_ref.shape[:2]
    pair_rows = x_ref.shape[3] // (beams // 2)
    table = table_ref[...]
    coefficients = spread(taps_ref)

    def loads(s):
        own = pl.ds(s * coarse, coarse)
        where = x_ref.at[s, :, pl.ds(EARLY * coarse, coarse)]
        return (
            pltpu.make_async_copy(where, x_buf.at[s], x_sem.at[s]),
            pltpu.make_async_copy(edge_ref.at[own], edge_buf.at[own], edge_sem.at[s]),
        )

    def stores(s):
        own = pl.ds(s * coarse, coarse)
        rows = pl.ds(HEAD, SPLIT - HEAD)
        return (
            pltpu.make_async_copy(out_buf.at[:, own], out_ref.at[:, own, rows], out_sem.at[s]),
            pltpu.make_async_copy(begin_buf.at[own], begin_ref.at[own], begin_sem.at[s]),
        )

    wait, finish, drain = grouped(channels, coarse, loads, stores)

    def make(c, slot, pair):
        rows = slice(pair * pair_rows, (pair + 1) * pair_rows)
        made = synth(x_buf[c // coarse, :, c % coarse, rows, :], table)
        for one in range(2):
            beam = 2 * pair + one
            interleave(lines[slot], made, beam, one, 0)
            lines[slot][beam, 2 * HALF : SPLIT, :] = edge_buf[c, beam].astype(jnp.float32)

    def use(c, slot, pair):
        for beam in (2 * pair, 2 * pair + 1):
            begin_buf[c, beam] = lines[slot][beam, :HEAD, :].astype(jnp.bfloat16)
            fir(lines[slot], beam, coefficients, HEAD, SPLIT - HEAD, out_buf, (beam, c))

    in_turn(channels, beams // 2, wait, make, use, finish)
    drain()


def middle(received, edge, table, taps, out, coarse):
    sources, blocks, _, rows, _ = received.shape
    beams, channels = out.shape[:2]
    anywhere = pl.BlockSpec(memory_space=pl.ANY)
    inside = pl.BlockSpec(memory_space=pltpu.VMEM)
    begin = (channels, beams, HEAD, LANES)
    return pl.pallas_call(
        functools.partial(middle_kernel, coarse),
        in_specs=[anywhere, anywhere, inside, inside, anywhere],
        out_specs=[anywhere, anywhere],
        out_shape=[jax.ShapeDtypeStruct(out.shape, out.dtype), jax.ShapeDtypeStruct(begin, jnp.bfloat16)],
        scratch_shapes=[
            pltpu.VMEM((sources, blocks, coarse, rows, LANES), jnp.bfloat16),
            pltpu.VMEM(edge.shape, jnp.bfloat16),
            pltpu.VMEM((beams, channels, SPLIT - HEAD, LANES), jnp.bfloat16),
            pltpu.VMEM(begin, jnp.bfloat16),
            pltpu.VMEM((beams, SPLIT, LANES), jnp.float32),
            pltpu.VMEM((beams, SPLIT, LANES), jnp.float32),
            pltpu.SemaphoreType.DMA((channels,)),
            pltpu.SemaphoreType.DMA((channels,)),
            pltpu.SemaphoreType.DMA((channels,)),
            pltpu.SemaphoreType.DMA((channels,)),
        ],
        input_output_aliases={4: 0},
        compiler_params=pltpu.CompilerParams(vmem_limit_bytes=VMEM),
        cost_estimate=pl.CostEstimate(
            flops=channels * beams * HALF * 2 * 256 * 256,
            bytes_accessed=2 * channels * beams * (4 * HALF + SPLIT) * LANES,
            transcendentals=0,
        ),
        name="middle",
    )(received, edge, table, taps, out)


def first_kernel(begin_ref, halo_ref, taps_ref, _, out_ref, *scratch):
    begin_buf, halo_buf, out_buf, lines_a, lines_b, tail, begin_sem, halo_sem, out_sem = scratch
    lines = (lines_a, lines_b)
    beams, channels = out_ref.shape[:2]
    start = 32
    coefficients = spread(taps_ref)

    size = channels // 4

    def loads(s):
        own = pl.ds(s * size, size)
        return (
            pltpu.make_async_copy(begin_ref.at[own], begin_buf.at[own], begin_sem.at[s]),
            pltpu.make_async_copy(halo_ref.at[own], halo_buf.at[own], halo_sem.at[s]),
        )

    def stores(s):
        own = pl.ds(s * size, size)
        return (pltpu.make_async_copy(out_buf.at[:, own], out_ref.at[:, own, pl.ds(0, HEAD)], out_sem.at[s]),)

    wait, finish, drain = grouped(channels, size, loads, stores)

    def make(c, slot, pair):
        if pair == 0:
            tail[...] = halo_buf[c].astype(jnp.float32)
        for beam in (2 * pair, 2 * pair + 1):
            lines[slot][beam, start - 2 * HALO : start, :] = tail[2 * HALO * beam : 2 * HALO * (beam + 1), :]
            lines[slot][beam, start : start + HEAD, :] = begin_buf[c, beam].astype(jnp.float32)

    def use(c, slot, pair):
        for beam in (2 * pair, 2 * pair + 1):
            fir(lines[slot], beam, coefficients, start, HEAD, out_buf, (beam, c))

    in_turn(channels, beams // 2, wait, make, use, finish)
    drain()


def first(begin, halo, taps, out):
    beams, channels = out.shape[:2]
    anywhere = pl.BlockSpec(memory_space=pl.ANY)
    inside = pl.BlockSpec(memory_space=pltpu.VMEM)
    return pl.pallas_call(
        first_kernel,
        in_specs=[anywhere, anywhere, inside, anywhere],
        out_specs=anywhere,
        out_shape=jax.ShapeDtypeStruct(out.shape, out.dtype),
        scratch_shapes=[
            pltpu.VMEM(begin.shape, jnp.bfloat16),
            pltpu.VMEM(halo.shape, jnp.bfloat16),
            pltpu.VMEM((beams, channels, HEAD, LANES), jnp.bfloat16),
            pltpu.VMEM((beams, 32 + HEAD, LANES), jnp.float32),
            pltpu.VMEM((beams, 32 + HEAD, LANES), jnp.float32),
            pltpu.VMEM(halo.shape[1:], jnp.float32),
            pltpu.SemaphoreType.DMA((channels,)),
            pltpu.SemaphoreType.DMA((channels,)),
            pltpu.SemaphoreType.DMA((channels,)),
        ],
        input_output_aliases={3: 0},
        compiler_params=pltpu.CompilerParams(vmem_limit_bytes=VMEM),
        cost_estimate=pl.CostEstimate(
            flops=channels * beams * HEAD * LANES * 24,
            bytes_accessed=2 * channels * beams * 3 * HEAD * LANES,
            transcendentals=0,
        ),
        name="first",
    )(begin, halo, taps, out)


def on_device(spectra, prototype):
    groups, blocks = lax.axis_size("beam"), lax.axis_size("tm")
    coarse, parts, fine, all_beams, _ = spectra.shape
    beams = all_beams // groups
    length = blocks * fine
    table = synth_table(length).reshape(parts, blocks, fine, 2 * length)
    table = table.transpose(1, 0, 2, 3).reshape(parts * length, 2 * length)
    packed = pack(spectra, UNITS, groups, blocks)
    moved = lax.all_to_all(packed, ("beam", "tm"), 0, 0, tiled=True)
    received = moved.reshape(groups, blocks, *moved.shape[1:])
    out, edge, halo = late(received, table, prototype, coarse, beams)
    halo = lax.ppermute(halo, "tm", [(i, i + 1) for i in range(blocks - 1)])
    out, begin = middle(received, edge, table, prototype, out, coarse)
    out = first(begin, halo, prototype, out)
    channels = groups * coarse
    out = out.reshape(beams, channels, 2 * HALF, 2, LANES).swapaxes(2, 3)
    return out.reshape(beams, channels, 2, 2 * HALF * LANES)


def solution(mesh):
    in_specs = (P("beam", None, "tm", None, None), P())
    out_specs = P("beam", None, None, "tm")
    return jax.shard_map(on_device, mesh=mesh, in_specs=in_specs, out_specs=out_specs, check_vma=False)
```

```python
import functools
import math

import jax
import jax.numpy as jnp
import numpy as np
from jax import lax
from jax.experimental import pallas as pl
from jax.experimental.pallas import tpu as pltpu
from jax.sharding import PartitionSpec as P

EARLY, LATE = 0, 1
UNITS = ((0, EARLY), (1, EARLY), (2, EARLY), (0, LATE), (1, LATE), (2, LATE))
LANES = 128
HALF = 64
EDGE = 16
HALO = 11
ROWS = 4 * HALF
SPLIT = 2 * (HALF + EDGE)
HEAD = 2 * EDGE
VMEM = 40 * 2**20


def synth_table(length, blocks):
    index = np.arange(length)
    angle = ((index[:, None] * index[None, :]) % length).astype(np.float32) * np.float32(2.0 * math.pi / length)
    cosine = np.cos(angle) / np.float32(math.sqrt(length))
    sine = np.sin(angle) / np.float32(math.sqrt(length))
    real_row = np.stack([cosine, sine], axis=1)
    imag_row = np.stack([-sine, cosine], axis=1)
    table = np.stack([real_row, imag_row], axis=0).reshape(2, blocks, length // blocks, 2 * length)
    return table.transpose(1, 0, 2, 3).reshape(2 * length, 2 * length).astype(jnp.bfloat16)


def row_order(parts, fine, beams):
    count = parts * fine * beams
    rows = np.arange(count).reshape(parts * fine, 2, beams // 4, 2).transpose(1, 3, 2, 0).reshape(count)
    return np.eye(count, dtype=np.float32)[rows].astype(jnp.bfloat16)


def pack_kernel(units, blocks, x_ref, order_ref, y_ref, x_buf, y_buf, x_sem, y_sem):
    channels = sorted({c for c, _ in units})
    _, parts, fine, all_beams, frames = x_ref.shape
    beams = 16
    strips = all_beams // beams
    rows = y_ref.shape[2]

    def load(i, g):
        where = (slice(None), slice(None), pl.ds(pl.multiple_of(g * beams, beams), beams), slice(None))
        return pltpu.make_async_copy(x_ref.at[(channels[i], *where)], x_buf.at[(i, *where)], x_sem.at[i, g])

    def store(u, g):
        where = (pl.ds(g * 2 * blocks, 2 * blocks), u)
        return pltpu.make_async_copy(y_buf.at[where], y_ref.at[where], y_sem.at[u, g])

    for i in range(len(channels)):
        for g in range(strips):
            load(i, g).start()
    order = order_ref[...]
    lower = lax.broadcasted_iota(jnp.int32, (rows, LANES), 1) < HALF

    for i, channel in enumerate(channels):
        own = [(u, h) for u, (c, h) in enumerate(units) if c == channel]

        def strip(g, carry):
            load(i, g).wait()
            for t in range(0, blocks, 2):
                lines = x_buf[i, :, :, pl.ds(pl.multiple_of(g * beams, beams), beams), t * LANES : (t + 2) * LANES]
                lines = lines.reshape(parts * fine * beams, 2 * LANES)
                moved = jnp.dot(order, lines, preferred_element_type=jnp.float32)
                for part in range(2):
                    for group in range(2):
                        block = moved[2 * group * rows : 2 * (group + 1) * rows, part * LANES : (part + 1) * LANES]
                        even, odd = block[:rows], pltpu.roll(block[rows:], HALF, 1)
                        for u, h in own:
                            made = jnp.where(lower, odd, even) if h == LATE else jnp.where(lower, even, odd)
                            y_buf[(2 * g + group) * blocks + t + part, u] = made.astype(jnp.bfloat16)
            for u, _ in own:
                store(u, g).start()
            return carry

        lax.fori_loop(0, strips, strip, 0)
    for u in range(len(units)):
        for g in range(strips):
            store(u, g).wait()


def pack(spectra, units, groups, blocks):
    coarse, parts, fine, beams, frames = spectra.shape
    rows = (beams // groups) // 2 * parts * fine
    strips = beams // 16
    channels = len({c for c, _ in units})
    order = jnp.asarray(row_order(parts, fine, 16))
    shape = (groups * blocks, len(units), rows, LANES)
    return pl.pallas_call(
        functools.partial(pack_kernel, units, blocks),
        in_specs=[pl.BlockSpec(memory_space=pl.ANY), pl.BlockSpec(memory_space=pltpu.VMEM)],
        out_specs=pl.BlockSpec(memory_space=pl.ANY),
        out_shape=jax.ShapeDtypeStruct(shape, jnp.bfloat16),
        scratch_shapes=[
            pltpu.VMEM((channels, parts, fine, beams, frames), jnp.bfloat16),
            pltpu.VMEM(shape, jnp.bfloat16),
            pltpu.SemaphoreType.DMA((channels, strips)),
            pltpu.SemaphoreType.DMA((len(units), strips)),
        ],
        compiler_params=pltpu.CompilerParams(vmem_limit_bytes=VMEM),
        cost_estimate=pl.CostEstimate(
            flops=channels * 2 * 256 * 256 * strips * frames,
            bytes_accessed=2 * channels * parts * fine * beams * frames + 2 * math.prod(shape),
            transcendentals=0,
        ),
        name="pack",
    )(spectra, order)


def synth(block, table):
    rows = block.shape[0] * block.shape[1]
    made = lax.dot_general(
        block.reshape(rows, LANES), table, (((0,), (0,)), ((), ())), preferred_element_type=jnp.float32
    )
    return made.astype(jnp.bfloat16).astype(jnp.float32)


def interleave(lines_ref, made, beam, one, start):
    for q in range(2):
        lines_ref[beam, pl.ds(start + q, HALF, stride=2), :] = made[
            one * HALF : (one + 1) * HALF, q * LANES : (q + 1) * LANES
        ]


def fir(lines_ref, beam, coefficients, start, count, out_ref, where):
    window = {}
    done = []
    for m in range(count // 8):
        total = None
        for j, coefficient in enumerate(coefficients):
            key = (m - j // 4, j % 4)
            if key not in window:
                first = start + 8 * key[0] - 2 * key[1]
                window[key] = lines_ref[beam, first : first + 8, :]
            term = coefficient * window[key]
            total = term if total is None else total + term
        done.append(total)
        if len(done) == 2:
            out_ref[(*where, pl.ds(8 * (m - 1), 16), slice(None))] = jnp.concatenate(done, axis=0).astype(jnp.bfloat16)
            done = []


def spread(taps_ref):
    return [jnp.broadcast_to(taps_ref[j : j + 1, :], (8, LANES)) for j in range(taps_ref.shape[0])]


def in_turn(count, pairs, wait, make, use, finish):
    wait(0)
    for pair in range(pairs):
        make(0, 0, pair)

    def two(step, carry):
        for slot in range(2):
            now = 2 * step + slot
            if slot == 0:
                wait(now + 1)
                later = now + 1
            else:
                later = jnp.minimum(now + 1, count - 1)

                @pl.when(now + 1 < count)
                def _():
                    wait(later)

            for pair in range(pairs):
                make(later, 1 - slot, pair)
                use(now, slot, pair)
            finish(now)
        return carry

    lax.fori_loop(0, count // 2, two, 0)


def grouped(count, size, loads, stores):
    for group in range(count // size):
        for copy in loads(group):
            copy.start()

    def wait(i):
        @pl.when(i % size == 0)
        def _():
            for copy in loads(i // size):
                copy.wait()

    def finish(i):
        @pl.when(i % size == size - 1)
        def _():
            for copy in stores(i // size):
                copy.start()

    def drain():
        for group in range(count // size):
            for copy in stores(group):
                copy.wait()

    return wait, finish, drain


def late_kernel(coarse, x_ref, table_ref, taps_ref, out_ref, edge_ref, halo_ref, *scratch):
    x_buf, out_buf, edge_buf, halo_buf, lines_a, lines_b, tail, x_sem, out_sem, edge_sem, halo_sem = scratch
    lines = (lines_a, lines_b)
    beams, channels = out_ref.shape[:2]
    pair_rows = x_ref.shape[3] // (beams // 2)
    table = table_ref[...]
    coefficients = spread(taps_ref)

    def loads(s):
        where = x_ref.at[s, :, pl.ds(LATE * coarse, coarse)]
        return (pltpu.make_async_copy(where, x_buf.at[s], x_sem.at[s]),)

    def stores(s):
        own = pl.ds(s * coarse, coarse)
        rows = pl.ds(SPLIT, ROWS - SPLIT)
        return (
            pltpu.make_async_copy(out_buf.at[:, own], out_ref.at[:, own, rows], out_sem.at[s]),
            pltpu.make_async_copy(edge_buf.at[own], edge_ref.at[own], edge_sem.at[s]),
            pltpu.make_async_copy(halo_buf.at[own], halo_ref.at[own], halo_sem.at[s]),
        )

    wait, send, drain = grouped(channels, coarse, loads, stores)

    def make(c, slot, pair):
        rows = slice(pair * pair_rows, (pair + 1) * pair_rows)
        made = synth(x_buf[c // coarse, :, c % coarse, rows, :], table)
        for one in range(2):
            interleave(lines[slot], made, 2 * pair + 1 - one, one, 0)

    def use(c, slot, pair):
        for beam in (2 * pair, 2 * pair + 1):
            edge_buf[c, beam] = lines[slot][beam, : 2 * EDGE, :].astype(jnp.bfloat16)
            tail[2 * HALO * beam : 2 * HALO * (beam + 1), :] = lines[slot][beam, 2 * (HALF - HALO) : 2 * HALF, :]
            fir(lines[slot], beam, coefficients, 2 * EDGE, ROWS - SPLIT, out_buf, (beam, c))

    def finish(c):
        halo_buf[c] = tail[...].astype(jnp.bfloat16)
        send(c)

    in_turn(channels, beams // 2, wait, make, use, finish)
    drain()


def late(received, table, taps, coarse, beams):
    sources, blocks, _, rows, _ = received.shape
    channels = sources * coarse
    anywhere = pl.BlockSpec(memory_space=pl.ANY)
    inside = pl.BlockSpec(memory_space=pltpu.VMEM)
    edge = (channels, beams, 2 * EDGE, LANES)
    halo = (channels, beams * 2 * HALO, LANES)
    return pl.pallas_call(
        functools.partial(late_kernel, coarse),
        in_specs=[anywhere, inside, inside],
        out_specs=[anywhere, anywhere, anywhere],
        out_shape=[
            jax.ShapeDtypeStruct((beams, channels, ROWS, LANES), jnp.bfloat16),
            jax.ShapeDtypeStruct(edge, jnp.bfloat16),
            jax.ShapeDtypeStruct(halo, jnp.bfloat16),
        ],
        scratch_shapes=[
            pltpu.VMEM((sources, blocks, coarse, rows, LANES), jnp.bfloat16),
            pltpu.VMEM((beams, channels, ROWS - SPLIT, LANES), jnp.bfloat16),
            pltpu.VMEM(edge, jnp.bfloat16),
            pltpu.VMEM(halo, jnp.bfloat16),
            pltpu.VMEM((beams, 2 * HALF, LANES), jnp.float32),
            pltpu.VMEM((beams, 2 * HALF, LANES), jnp.float32),
            pltpu.VMEM((beams * 2 * HALO, LANES), jnp.float32),
            pltpu.SemaphoreType.DMA((channels,)),
            pltpu.SemaphoreType.DMA((channels,)),
            pltpu.SemaphoreType.DMA((channels,)),
            pltpu.SemaphoreType.DMA((channels,)),
        ],
        compiler_params=pltpu.CompilerParams(vmem_limit_bytes=VMEM),
        cost_estimate=pl.CostEstimate(
            flops=channels * beams * HALF * 2 * 256 * 256,
            bytes_accessed=2 * channels * beams * (4 * HALF + ROWS - SPLIT) * LANES,
            transcendentals=0,
        ),
        name="late",
    )(received, table, taps)


def middle_kernel(coarse, x_ref, edge_ref, table_ref, taps_ref, _, out_ref, begin_ref, *scratch):
    x_buf, edge_buf, out_buf, begin_buf, lines_a, lines_b, x_sem, edge_sem, out_sem, begin_sem = scratch
    lines = (lines_a, lines_b)
    beams, channels = out_ref.shape[:2]
    pair_rows = x_ref.shape[3] // (beams // 2)
    table = table_ref[...]
    coefficients = spread(taps_ref)

    def loads(s):
        own = pl.ds(s * coarse, coarse)
        where = x_ref.at[s, :, pl.ds(EARLY * coarse, coarse)]
        return (
            pltpu.make_async_copy(where, x_buf.at[s], x_sem.at[s]),
            pltpu.make_async_copy(edge_ref.at[own], edge_buf.at[own], edge_sem.at[s]),
        )

    def stores(s):
        own = pl.ds(s * coarse, coarse)
        rows = pl.ds(HEAD, SPLIT - HEAD)
        return (
            pltpu.make_async_copy(out_buf.at[:, own], out_ref.at[:, own, rows], out_sem.at[s]),
            pltpu.make_async_copy(begin_buf.at[own], begin_ref.at[own], begin_sem.at[s]),
        )

    wait, finish, drain = grouped(channels, coarse, loads, stores)

    def make(c, slot, pair):
        rows = slice(pair * pair_rows, (pair + 1) * pair_rows)
        made = synth(x_buf[c // coarse, :, c % coarse, rows, :], table)
        for one in range(2):
            beam = 2 * pair + one
            interleave(lines[slot], made, beam, one, 0)
            lines[slot][beam, 2 * HALF : SPLIT, :] = edge_buf[c, beam].astype(jnp.float32)

    def use(c, slot, pair):
        for beam in (2 * pair, 2 * pair + 1):
            begin_buf[c, beam] = lines[slot][beam, :HEAD, :].astype(jnp.bfloat16)
            fir(lines[slot], beam, coefficients, HEAD, SPLIT - HEAD, out_buf, (beam, c))

    in_turn(channels, beams // 2, wait, make, use, finish)
    drain()


def middle(received, edge, table, taps, out, coarse):
    sources, blocks, _, rows, _ = received.shape
    beams, channels = out.shape[:2]
    anywhere = pl.BlockSpec(memory_space=pl.ANY)
    inside = pl.BlockSpec(memory_space=pltpu.VMEM)
    begin = (channels, beams, HEAD, LANES)
    return pl.pallas_call(
        functools.partial(middle_kernel, coarse),
        in_specs=[anywhere, anywhere, inside, inside, anywhere],
        out_specs=[anywhere, anywhere],
        out_shape=[jax.ShapeDtypeStruct(out.shape, out.dtype), jax.ShapeDtypeStruct(begin, jnp.bfloat16)],
        scratch_shapes=[
            pltpu.VMEM((sources, blocks, coarse, rows, LANES), jnp.bfloat16),
            pltpu.VMEM(edge.shape, jnp.bfloat16),
            pltpu.VMEM((beams, channels, SPLIT - HEAD, LANES), jnp.bfloat16),
            pltpu.VMEM(begin, jnp.bfloat16),
            pltpu.VMEM((beams, SPLIT, LANES), jnp.float32),
            pltpu.VMEM((beams, SPLIT, LANES), jnp.float32),
            pltpu.SemaphoreType.DMA((channels,)),
            pltpu.SemaphoreType.DMA((channels,)),
            pltpu.SemaphoreType.DMA((channels,)),
            pltpu.SemaphoreType.DMA((channels,)),
        ],
        input_output_aliases={4: 0},
        compiler_params=pltpu.CompilerParams(vmem_limit_bytes=VMEM),
        cost_estimate=pl.CostEstimate(
            flops=channels * beams * HALF * 2 * 256 * 256,
            bytes_accessed=2 * channels * beams * (4 * HALF + SPLIT) * LANES,
            transcendentals=0,
        ),
        name="middle",
    )(received, edge, table, taps, out)


def first_kernel(begin_ref, halo_ref, taps_ref, _, out_ref, *scratch):
    begin_buf, halo_buf, out_buf, lines_a, lines_b, tail, begin_sem, halo_sem, out_sem = scratch
    lines = (lines_a, lines_b)
    beams, channels = out_ref.shape[:2]
    start = 32
    coefficients = spread(taps_ref)

    size = channels // 4

    def loads(s):
        own = pl.ds(s * size, size)
        return (
            pltpu.make_async_copy(begin_ref.at[own], begin_buf.at[own], begin_sem.at[s]),
            pltpu.make_async_copy(halo_ref.at[own], halo_buf.at[own], halo_sem.at[s]),
        )

    def stores(s):
        own = pl.ds(s * size, size)
        return (pltpu.make_async_copy(out_buf.at[:, own], out_ref.at[:, own, pl.ds(0, HEAD)], out_sem.at[s]),)

    wait, finish, drain = grouped(channels, size, loads, stores)

    def make(c, slot, pair):
        if pair == 0:
            tail[...] = halo_buf[c].astype(jnp.float32)
        for beam in (2 * pair, 2 * pair + 1):
            lines[slot][beam, start - 2 * HALO : start, :] = tail[2 * HALO * beam : 2 * HALO * (beam + 1), :]
            lines[slot][beam, start : start + HEAD, :] = begin_buf[c, beam].astype(jnp.float32)

    def use(c, slot, pair):
        for beam in (2 * pair, 2 * pair + 1):
            fir(lines[slot], beam, coefficients, start, HEAD, out_buf, (beam, c))

    in_turn(channels, beams // 2, wait, make, use, finish)
    drain()


def first(begin, halo, taps, out):
    beams, channels = out.shape[:2]
    anywhere = pl.BlockSpec(memory_space=pl.ANY)
    inside = pl.BlockSpec(memory_space=pltpu.VMEM)
    return pl.pallas_call(
        first_kernel,
        in_specs=[anywhere, anywhere, inside, anywhere],
        out_specs=anywhere,
        out_shape=jax.ShapeDtypeStruct(out.shape, out.dtype),
        scratch_shapes=[
            pltpu.VMEM(begin.shape, jnp.bfloat16),
            pltpu.VMEM(halo.shape, jnp.bfloat16),
            pltpu.VMEM((beams, channels, HEAD, LANES), jnp.bfloat16),
            pltpu.VMEM((beams, 32 + HEAD, LANES), jnp.float32),
            pltpu.VMEM((beams, 32 + HEAD, LANES), jnp.float32),
            pltpu.VMEM(halo.shape[1:], jnp.float32),
            pltpu.SemaphoreType.DMA((channels,)),
            pltpu.SemaphoreType.DMA((channels,)),
            pltpu.SemaphoreType.DMA((channels,)),
        ],
        input_output_aliases={3: 0},
        compiler_params=pltpu.CompilerParams(vmem_limit_bytes=VMEM),
        cost_estimate=pl.CostEstimate(
            flops=channels * beams * HEAD * LANES * 24,
            bytes_accessed=2 * channels * beams * 3 * HEAD * LANES,
            transcendentals=0,
        ),
        name="first",
    )(begin, halo, taps, out)


def on_device(spectra, prototype):
    groups, blocks = lax.axis_size("beam"), lax.axis_size("tm")
    coarse, parts, fine, all_beams, _ = spectra.shape
    beams = all_beams // groups
    length = blocks * fine
    table = jnp.asarray(synth_table(length, blocks))
    packed = pack(spectra, UNITS, groups, blocks)
    moved = lax.all_to_all(packed, ("beam", "tm"), 0, 0, tiled=True)
    received = moved.reshape(groups, blocks, *moved.shape[1:])
    out, edge, halo = late(received, table, prototype, coarse, beams)
    halo = lax.ppermute(halo, "tm", [(i, i + 1) for i in range(blocks - 1)])
    out, begin = middle(received, edge, table, prototype, out, coarse)
    out = first(begin, halo, prototype, out)
    channels = groups * coarse
    out = out.reshape(beams, channels, 2 * HALF, 2, LANES).swapaxes(2, 3)
    return out.reshape(beams, channels, 2, 2 * HALF * LANES)


def solution(mesh):
    in_specs = (P("beam", None, "tm", None, None), P())
    out_specs = P("beam", None, None, "tm")
    return jax.shard_map(on_device, mesh=mesh, in_specs=in_specs, out_specs=out_specs, check_vma=False)
```

```python
import functools
import math

import jax
import jax.numpy as jnp
import numpy as np
from jax import lax
from jax.experimental import pallas as pl
from jax.experimental.pallas import tpu as pltpu
from jax.sharding import PartitionSpec as P

EARLY, LATE = 0, 1
UNITS = ((0, EARLY), (1, EARLY), (2, EARLY), (0, LATE), (1, LATE), (2, LATE))
LANES = 128
HALF = 64
EDGE = 16
HALO = 11
ROWS = 4 * HALF
SPLIT = 2 * (HALF + EDGE)
HEAD = 2 * EDGE
VMEM = 40 * 2**20


def synth_table(length, blocks):
    index = np.arange(length)
    angle = ((index[:, None] * index[None, :]) % length).astype(np.float32) * np.float32(2.0 * math.pi / length)
    cosine = np.cos(angle) / np.float32(math.sqrt(length))
    sine = np.sin(angle) / np.float32(math.sqrt(length))
    real_row = np.stack([cosine, sine], axis=1)
    imag_row = np.stack([-sine, cosine], axis=1)
    table = np.stack([real_row, imag_row], axis=0).reshape(2, blocks, length // blocks, 2 * length)
    return table.transpose(1, 0, 2, 3).reshape(2 * length, 2 * length).astype(jnp.bfloat16)


def row_order(parts, fine, beams):
    count = parts * fine * beams
    rows = np.arange(count).reshape(parts * fine, 2, beams // 4, 2).transpose(1, 3, 2, 0).reshape(count)
    return np.eye(count, dtype=np.float32)[rows].astype(jnp.bfloat16)


def pack_kernel(units, blocks, x_ref, order_ref, y_ref, x_buf, y_buf, x_sem, y_sem):
    channels = sorted({c for c, _ in units})
    _, parts, fine, all_beams, frames = x_ref.shape
    beams = 16
    strips = all_beams // beams
    rows = y_ref.shape[2]

    def load(i, g):
        where = (slice(None), slice(None), pl.ds(pl.multiple_of(g * beams, beams), beams), slice(None))
        return pltpu.make_async_copy(x_ref.at[(channels[i], *where)], x_buf.at[(i, *where)], x_sem.at[i, g])

    def store(u, g):
        where = (pl.ds(g * 2 * blocks, 2 * blocks), u)
        return pltpu.make_async_copy(y_buf.at[where], y_ref.at[where], y_sem.at[u, g])

    for i in range(len(channels)):
        for g in range(strips):
            load(i, g).start()
    order = order_ref[...]
    lower = lax.broadcasted_iota(jnp.int32, (rows, LANES), 1) < HALF

    for i, channel in enumerate(channels):
        own = [(u, h) for u, (c, h) in enumerate(units) if c == channel]

        def strip(g, carry):
            load(i, g).wait()
            for t in range(0, blocks, 2):
                lines = x_buf[i, :, :, pl.ds(pl.multiple_of(g * beams, beams), beams), t * LANES : (t + 2) * LANES]
                lines = lines.reshape(parts * fine * beams, 2 * LANES)
                moved = jnp.dot(order, lines, preferred_element_type=jnp.float32)
                for part in range(2):
                    for group in range(2):
                        block = moved[2 * group * rows : 2 * (group + 1) * rows, part * LANES : (part + 1) * LANES]
                        even, odd = block[:rows], pltpu.roll(block[rows:], HALF, 1)
                        for u, h in own:
                            made = jnp.where(lower, odd, even) if h == LATE else jnp.where(lower, even, odd)
                            y_buf[(2 * g + group) * blocks + t + part, u] = made.astype(jnp.bfloat16)
            for u, _ in own:
                store(u, g).start()
            return carry

        lax.fori_loop(0, strips, strip, 0)
    for u in range(len(units)):
        for g in range(strips):
            store(u, g).wait()


def pack(spectra, units, groups, blocks):
    coarse, parts, fine, beams, frames = spectra.shape
    rows = (beams // groups) // 2 * parts * fine
    strips = beams // 16
    channels = len({c for c, _ in units})
    order = jnp.asarray(row_order(parts, fine, 16))
    shape = (groups * blocks, len(units), rows, LANES)
    return pl.pallas_call(
        functools.partial(pack_kernel, units, blocks),
        in_specs=[pl.BlockSpec(memory_space=pl.ANY), pl.BlockSpec(memory_space=pltpu.VMEM)],
        out_specs=pl.BlockSpec(memory_space=pl.ANY),
        out_shape=jax.ShapeDtypeStruct(shape, jnp.bfloat16),
        scratch_shapes=[
            pltpu.VMEM((channels, parts, fine, beams, frames), jnp.bfloat16),
            pltpu.VMEM(shape, jnp.bfloat16),
            pltpu.SemaphoreType.DMA((channels, strips)),
            pltpu.SemaphoreType.DMA((len(units), strips)),
        ],
        compiler_params=pltpu.CompilerParams(vmem_limit_bytes=VMEM),
        cost_estimate=pl.CostEstimate(
            flops=channels * 2 * 256 * 256 * strips * frames,
            bytes_accessed=2 * channels * parts * fine * beams * frames + 2 * math.prod(shape),
            transcendentals=0,
        ),
        name="pack",
    )(spectra, order)


def synth(block, table):
    rows = block.shape[0] * block.shape[1]
    made = lax.dot_general(
        block.reshape(rows, LANES), table, (((0,), (0,)), ((), ())), preferred_element_type=jnp.float32
    )
    return made.astype(jnp.bfloat16).astype(jnp.float32)


def interleave(lines_ref, made, beam, one, start):
    for q in range(2):
        lines_ref[beam, pl.ds(start + q, HALF, stride=2), :] = made[
            one * HALF : (one + 1) * HALF, q * LANES : (q + 1) * LANES
        ]


def fir(lines_ref, beam, coefficients, start, count, out_ref, where):
    window = {}
    done = []
    for m in range(count // 8):
        total = None
        for j, coefficient in enumerate(coefficients):
            key = (m - j // 4, j % 4)
            if key not in window:
                first = start + 8 * key[0] - 2 * key[1]
                window[key] = lines_ref[beam, first : first + 8, :]
            term = coefficient * window[key]
            total = term if total is None else total + term
        done.append(total)
        if len(done) == 2:
            out_ref[(*where, pl.ds(8 * (m - 1), 16), slice(None))] = jnp.concatenate(done, axis=0).astype(jnp.bfloat16)
            done = []


def spread(taps_ref):
    return [jnp.broadcast_to(taps_ref[j : j + 1, :], (8, LANES)) for j in range(taps_ref.shape[0])]


def in_turn(count, pairs, wait, make, use, finish):
    wait(0)
    for pair in range(pairs):
        make(0, 0, pair)

    def two(step, carry):
        for slot in range(2):
            now = 2 * step + slot
            if slot == 0:
                wait(now + 1)
                later = now + 1
            else:
                later = jnp.minimum(now + 1, count - 1)

                @pl.when(now + 1 < count)
                def _():
                    wait(later)

            for pair in range(pairs):
                make(later, 1 - slot, pair)
                use(now, slot, pair)
            finish(now)
        return carry

    lax.fori_loop(0, count // 2, two, 0)


def grouped(count, size, loads, stores):
    for group in range(count // size):
        for copy in loads(group):
            copy.start()

    def wait(i):
        @pl.when(i % size == 0)
        def _():
            for copy in loads(i // size):
                copy.wait()

    def finish(i):
        @pl.when(i % size == size - 1)
        def _():
            for copy in stores(i // size):
                copy.start()

    def drain():
        for group in range(count // size):
            for copy in stores(group):
                copy.wait()

    return wait, finish, drain


def late_kernel(coarse, x_ref, table_ref, taps_ref, out_ref, edge_ref, halo_ref, *scratch):
    x_buf, out_buf, lines_a, lines_b, tail, x_sem, out_sem = scratch
    lines = (lines_a, lines_b)
    beams, channels = out_ref.shape[:2]
    pair_rows = x_ref.shape[3] // (beams // 2)
    table = table_ref[...]
    coefficients = spread(taps_ref)

    def loads(s):
        where = x_ref.at[s, :, pl.ds(LATE * coarse, coarse)]
        return (pltpu.make_async_copy(where, x_buf.at[s], x_sem.at[s]),)

    def stores(s):
        own = pl.ds(s * coarse, coarse)
        rows = pl.ds(SPLIT, ROWS - SPLIT)
        return (pltpu.make_async_copy(out_buf.at[:, own], out_ref.at[:, own, rows], out_sem.at[s]),)

    wait, send, drain = grouped(channels, coarse, loads, stores)

    def make(c, slot, pair):
        rows = slice(pair * pair_rows, (pair + 1) * pair_rows)
        made = synth(x_buf[c // coarse, :, c % coarse, rows, :], table)
        for one in range(2):
            interleave(lines[slot], made, 2 * pair + 1 - one, one, 0)

    def use(c, slot, pair):
        for beam in (2 * pair, 2 * pair + 1):
            edge_ref[c, beam] = lines[slot][beam, : 2 * EDGE, :].astype(jnp.bfloat16)
            tail[2 * HALO * beam : 2 * HALO * (beam + 1), :] = lines[slot][beam, 2 * (HALF - HALO) : 2 * HALF, :]
            fir(lines[slot], beam, coefficients, 2 * EDGE, ROWS - SPLIT, out_buf, (beam, c))

    def finish(c):
        halo_ref[c] = tail[...].astype(jnp.bfloat16)
        send(c)

    in_turn(channels, beams // 2, wait, make, use, finish)
    drain()


def late(received, table, taps, coarse, beams):
    sources, blocks, _, rows, _ = received.shape
    channels = sources * coarse
    anywhere = pl.BlockSpec(memory_space=pl.ANY)
    inside = pl.BlockSpec(memory_space=pltpu.VMEM)
    edge = (channels, beams, 2 * EDGE, LANES)
    halo = (channels, beams * 2 * HALO, LANES)
    return pl.pallas_call(
        functools.partial(late_kernel, coarse),
        in_specs=[anywhere, inside, inside],
        out_specs=[anywhere, inside, inside],
        out_shape=[
            jax.ShapeDtypeStruct((beams, channels, ROWS, LANES), jnp.bfloat16),
            jax.ShapeDtypeStruct(edge, jnp.bfloat16),
            jax.ShapeDtypeStruct(halo, jnp.bfloat16),
        ],
        scratch_shapes=[
            pltpu.VMEM((sources, blocks, coarse, rows, LANES), jnp.bfloat16),
            pltpu.VMEM((beams, channels, ROWS - SPLIT, LANES), jnp.bfloat16),
            pltpu.VMEM((beams, 2 * HALF, LANES), jnp.float32),
            pltpu.VMEM((beams, 2 * HALF, LANES), jnp.float32),
            pltpu.VMEM((beams * 2 * HALO, LANES), jnp.float32),
            pltpu.SemaphoreType.DMA((sources,)),
            pltpu.SemaphoreType.DMA((sources,)),
        ],
        compiler_params=pltpu.CompilerParams(vmem_limit_bytes=VMEM),
        cost_estimate=pl.CostEstimate(
            flops=channels * beams * HALF * 2 * 256 * 256,
            bytes_accessed=2 * channels * beams * (4 * HALF + ROWS - SPLIT) * LANES,
            transcendentals=0,
        ),
        name="late",
    )(received, table, taps)


def middle_kernel(coarse, x_ref, edge_ref, table_ref, taps_ref, _, out_ref, begin_ref, *scratch):
    x_buf, out_buf, lines_a, lines_b, x_sem, out_sem = scratch
    lines = (lines_a, lines_b)
    beams, channels = out_ref.shape[:2]
    pair_rows = x_ref.shape[3] // (beams // 2)
    table = table_ref[...]
    coefficients = spread(taps_ref)

    def loads(s):
        where = x_ref.at[s, :, pl.ds(EARLY * coarse, coarse)]
        return (pltpu.make_async_copy(where, x_buf.at[s], x_sem.at[s]),)

    def stores(s):
        own = pl.ds(s * coarse, coarse)
        rows = pl.ds(HEAD, SPLIT - HEAD)
        return (pltpu.make_async_copy(out_buf.at[:, own], out_ref.at[:, own, rows], out_sem.at[s]),)

    wait, finish, drain = grouped(channels, coarse, loads, stores)

    def make(c, slot, pair):
        rows = slice(pair * pair_rows, (pair + 1) * pair_rows)
        made = synth(x_buf[c // coarse, :, c % coarse, rows, :], table)
        for one in range(2):
            beam = 2 * pair + one
            interleave(lines[slot], made, beam, one, 0)
            lines[slot][beam, 2 * HALF : SPLIT, :] = edge_ref[c, beam].astype(jnp.float32)

    def use(c, slot, pair):
        for beam in (2 * pair, 2 * pair + 1):
            begin_ref[c, beam] = lines[slot][beam, :HEAD, :].astype(jnp.bfloat16)
            fir(lines[slot], beam, coefficients, HEAD, SPLIT - HEAD, out_buf, (beam, c))

    in_turn(channels, beams // 2, wait, make, use, finish)
    drain()


def middle(received, edge, table, taps, out, coarse):
    sources, blocks, _, rows, _ = received.shape
    beams, channels = out.shape[:2]
    anywhere = pl.BlockSpec(memory_space=pl.ANY)
    inside = pl.BlockSpec(memory_space=pltpu.VMEM)
    begin = (channels, beams, HEAD, LANES)
    return pl.pallas_call(
        functools.partial(middle_kernel, coarse),
        in_specs=[anywhere, inside, inside, inside, anywhere],
        out_specs=[anywhere, inside],
        out_shape=[jax.ShapeDtypeStruct(out.shape, out.dtype), jax.ShapeDtypeStruct(begin, jnp.bfloat16)],
        scratch_shapes=[
            pltpu.VMEM((sources, blocks, coarse, rows, LANES), jnp.bfloat16),
            pltpu.VMEM((beams, channels, SPLIT - HEAD, LANES), jnp.bfloat16),
            pltpu.VMEM((beams, SPLIT, LANES), jnp.float32),
            pltpu.VMEM((beams, SPLIT, LANES), jnp.float32),
            pltpu.SemaphoreType.DMA((sources,)),
            pltpu.SemaphoreType.DMA((sources,)),
        ],
        input_output_aliases={4: 0},
        compiler_params=pltpu.CompilerParams(vmem_limit_bytes=VMEM),
        cost_estimate=pl.CostEstimate(
            flops=channels * beams * HALF * 2 * 256 * 256,
            bytes_accessed=2 * channels * beams * (4 * HALF + SPLIT) * LANES,
            transcendentals=0,
        ),
        name="middle",
    )(received, edge, table, taps, out)


def first_kernel(begin_ref, halo_ref, taps_ref, _, out_ref, *scratch):
    out_buf, lines_a, lines_b, tail, out_sem = scratch
    lines = (lines_a, lines_b)
    beams, channels = out_ref.shape[:2]
    start = 32
    coefficients = spread(taps_ref)

    size = channels // 4

    def loads(s):
        return ()

    def stores(s):
        own = pl.ds(s * size, size)
        return (pltpu.make_async_copy(out_buf.at[:, own], out_ref.at[:, own, pl.ds(0, HEAD)], out_sem.at[s]),)

    wait, finish, drain = grouped(channels, size, loads, stores)

    def make(c, slot, pair):
        if pair == 0:
            tail[...] = halo_ref[c].astype(jnp.float32)
        for beam in (2 * pair, 2 * pair + 1):
            lines[slot][beam, start - 2 * HALO : start, :] = tail[2 * HALO * beam : 2 * HALO * (beam + 1), :]
            lines[slot][beam, start : start + HEAD, :] = begin_ref[c, beam].astype(jnp.float32)

    def use(c, slot, pair):
        for beam in (2 * pair, 2 * pair + 1):
            fir(lines[slot], beam, coefficients, start, HEAD, out_buf, (beam, c))

    in_turn(channels, beams // 2, wait, make, use, finish)
    drain()


def first(begin, halo, taps, out):
    beams, channels = out.shape[:2]
    anywhere = pl.BlockSpec(memory_space=pl.ANY)
    inside = pl.BlockSpec(memory_space=pltpu.VMEM)
    return pl.pallas_call(
        first_kernel,
        in_specs=[inside, inside, inside, anywhere],
        out_specs=anywhere,
        out_shape=jax.ShapeDtypeStruct(out.shape, out.dtype),
        scratch_shapes=[
            pltpu.VMEM((beams, channels, HEAD, LANES), jnp.bfloat16),
            pltpu.VMEM((beams, 32 + HEAD, LANES), jnp.float32),
            pltpu.VMEM((beams, 32 + HEAD, LANES), jnp.float32),
            pltpu.VMEM(halo.shape[1:], jnp.float32),
            pltpu.SemaphoreType.DMA((4,)),
        ],
        input_output_aliases={3: 0},
        compiler_params=pltpu.CompilerParams(vmem_limit_bytes=VMEM),
        cost_estimate=pl.CostEstimate(
            flops=channels * beams * HEAD * LANES * 24,
            bytes_accessed=2 * channels * beams * 3 * HEAD * LANES,
            transcendentals=0,
        ),
        name="first",
    )(begin, halo, taps, out)


def on_device(spectra, prototype):
    groups, blocks = lax.axis_size("beam"), lax.axis_size("tm")
    coarse, parts, fine, all_beams, _ = spectra.shape
    beams = all_beams // groups
    length = blocks * fine
    table = jnp.asarray(synth_table(length, blocks))
    packed = pack(spectra, UNITS, groups, blocks)
    moved = lax.all_to_all(packed, ("beam", "tm"), 0, 0, tiled=True)
    received = moved.reshape(groups, blocks, *moved.shape[1:])
    out, edge, halo = late(received, table, prototype, coarse, beams)
    halo = lax.ppermute(halo, "tm", [(i, i + 1) for i in range(blocks - 1)])
    out, begin = middle(received, edge, table, prototype, out, coarse)
    out = first(begin, halo, prototype, out)
    channels = groups * coarse
    out = out.reshape(beams, channels, 2 * HALF, 2, LANES).swapaxes(2, 3)
    return out.reshape(beams, channels, 2, 2 * HALF * LANES)


def solution(mesh):
    in_specs = (P("beam", None, "tm", None, None), P())
    out_specs = P("beam", None, None, "tm")
    return jax.shard_map(on_device, mesh=mesh, in_specs=in_specs, out_specs=out_specs, check_vma=False)
```

```python
import functools
import math

import jax
import jax.numpy as jnp
import numpy as np
from jax import lax
from jax.experimental import pallas as pl
from jax.experimental.pallas import tpu as pltpu
from jax.sharding import PartitionSpec as P

EARLY, LATE = 0, 1
UNITS = ((0, EARLY), (1, EARLY), (2, EARLY), (0, LATE), (1, LATE), (2, LATE))
LANES = 128
HALF = 64
EDGE = 16
HALO = 11
ROWS = 4 * HALF
SPLIT = 2 * (HALF + EDGE)
HEAD = 2 * EDGE
VMEM = 40 * 2**20


def synth_table(length, blocks):
    index = np.arange(length)
    angle = ((index[:, None] * index[None, :]) % length).astype(np.float32) * np.float32(2.0 * math.pi / length)
    cosine = np.cos(angle) / np.float32(math.sqrt(length))
    sine = np.sin(angle) / np.float32(math.sqrt(length))
    real_row = np.stack([cosine, sine], axis=1)
    imag_row = np.stack([-sine, cosine], axis=1)
    table = np.stack([real_row, imag_row], axis=0).reshape(2, blocks, length // blocks, 2 * length)
    return table.transpose(1, 0, 2, 3).reshape(2 * length, 2 * length).astype(jnp.bfloat16)


def pack_kernel(units, blocks, x_ref, y_ref, x_buf, y_buf, x_sem, y_sem):
    channels = sorted({c for c, _ in units})
    _, parts, fine, all_beams, frames = x_ref.shape
    beams = 16
    strips = all_beams // beams
    rows = y_ref.shape[2]

    def load(i, g):
        where = (slice(None), slice(None), pl.ds(pl.multiple_of(g * beams, beams), beams), slice(None))
        return pltpu.make_async_copy(x_ref.at[(channels[i], *where)], x_buf.at[(i, *where)], x_sem.at[i, g])

    def store(u, g):
        where = (pl.ds(g * 2 * blocks, 2 * blocks), u)
        return pltpu.make_async_copy(y_buf.at[where], y_ref.at[where], y_sem.at[u, g])

    for i in range(len(channels)):
        for g in range(strips):
            load(i, g).start()
    count = fine * beams
    row = lax.broadcasted_iota(jnp.int32, (count, count), 0)
    column = lax.broadcasted_iota(jnp.int32, (count, count), 1)
    pairs = beams // 4
    beam = row // (2 * pairs * fine) * (2 * pairs) + row // fine % pairs * 2 + row // (pairs * fine) % 2
    order = (column == row % fine * beams + beam).astype(jnp.bfloat16)
    lower = lax.broadcasted_iota(jnp.int32, (rows, LANES), 1) < HALF

    for i, channel in enumerate(channels):
        own = [(u, h) for u, (c, h) in enumerate(units) if c == channel]

        def strip(g, carry):
            load(i, g).wait()
            for t in range(0, blocks, 2):
                lines = x_buf[i, :, :, pl.ds(pl.multiple_of(g * beams, beams), beams), t * LANES : (t + 2) * LANES]
                moved = [
                    jnp.dot(order, lines[p].reshape(fine * beams, 2 * LANES), preferred_element_type=jnp.float32)
                    for p in range(parts)
                ]
                for part in range(2):
                    for group in range(2):
                        base = group * (rows)
                        lanes = slice(part * LANES, (part + 1) * LANES)
                        even, odd = [], []
                        for pair in range(rows // (parts * fine)):
                            for p in range(parts):
                                first = base + pair * fine
                                even.append(moved[p][first : first + fine, lanes])
                                first = base + rows // 2 + pair * fine
                                odd.append(moved[p][first : first + fine, lanes])
                        even = jnp.concatenate(even, axis=0)
                        odd = pltpu.roll(jnp.concatenate(odd, axis=0), HALF, 1)
                        for u, h in own:
                            made = jnp.where(lower, odd, even) if h == LATE else jnp.where(lower, even, odd)
                            y_buf[(2 * g + group) * blocks + t + part, u] = made.astype(jnp.bfloat16)
            for u, _ in own:
                store(u, g).start()
            return carry

        lax.fori_loop(0, strips, strip, 0)
    for u in range(len(units)):
        for g in range(strips):
            store(u, g).wait()


def pack(spectra, units, groups, blocks):
    coarse, parts, fine, beams, frames = spectra.shape
    rows = (beams // groups) // 2 * parts * fine
    strips = beams // 16
    channels = len({c for c, _ in units})
    shape = (groups * blocks, len(units), rows, LANES)
    return pl.pallas_call(
        functools.partial(pack_kernel, units, blocks),
        in_specs=[pl.BlockSpec(memory_space=pl.ANY)],
        out_specs=pl.BlockSpec(memory_space=pl.ANY),
        out_shape=jax.ShapeDtypeStruct(shape, jnp.bfloat16),
        scratch_shapes=[
            pltpu.VMEM((channels, parts, fine, beams, frames), jnp.bfloat16),
            pltpu.VMEM(shape, jnp.bfloat16),
            pltpu.SemaphoreType.DMA((channels, strips)),
            pltpu.SemaphoreType.DMA((len(units), strips)),
        ],
        compiler_params=pltpu.CompilerParams(vmem_limit_bytes=VMEM),
        cost_estimate=pl.CostEstimate(
            flops=channels * 2 * 256 * 256 * strips * frames,
            bytes_accessed=2 * channels * parts * fine * beams * frames + 2 * math.prod(shape),
            transcendentals=0,
        ),
        name="pack",
    )(spectra)


def synth(block, table):
    rows = block.shape[0] * block.shape[1]
    made = lax.dot_general(
        block.reshape(rows, LANES), table, (((0,), (0,)), ((), ())), preferred_element_type=jnp.float32
    )
    return made.astype(jnp.bfloat16).astype(jnp.float32)


def interleave(lines_ref, made, beam, one, start):
    for q in range(2):
        lines_ref[beam, pl.ds(start + q, HALF, stride=2), :] = made[
            one * HALF : (one + 1) * HALF, q * LANES : (q + 1) * LANES
        ]


def fir(lines_ref, beam, coefficients, start, count, out_ref, where):
    window = {}
    done = []
    for m in range(count // 8):
        total = None
        for j, coefficient in enumerate(coefficients):
            key = (m - j // 4, j % 4)
            if key not in window:
                first = start + 8 * key[0] - 2 * key[1]
                window[key] = lines_ref[beam, first : first + 8, :]
            term = coefficient * window[key]
            total = term if total is None else total + term
        done.append(total)
        if len(done) == 2:
            out_ref[(*where, pl.ds(8 * (m - 1), 16), slice(None))] = jnp.concatenate(done, axis=0).astype(jnp.bfloat16)
            done = []


def spread(taps_ref):
    return [jnp.broadcast_to(taps_ref[j : j + 1, :], (8, LANES)) for j in range(taps_ref.shape[0])]


def in_turn(count, pairs, wait, make, use, finish):
    wait(0)
    for pair in range(pairs):
        make(0, 0, pair)

    def two(step, carry):
        for slot in range(2):
            now = 2 * step + slot
            if slot == 0:
                wait(now + 1)
                later = now + 1
            else:
                later = jnp.minimum(now + 1, count - 1)

                @pl.when(now + 1 < count)
                def _():
                    wait(later)

            for pair in range(pairs):
                make(later, 1 - slot, pair)
                use(now, slot, pair)
            finish(now)
        return carry

    lax.fori_loop(0, count // 2, two, 0)


def grouped(count, size, loads, stores):
    for group in range(count // size):
        for copy in loads(group):
            copy.start()

    def wait(i):
        @pl.when(i % size == 0)
        def _():
            for copy in loads(i // size):
                copy.wait()

    def finish(i):
        @pl.when(i % size == size - 1)
        def _():
            for copy in stores(i // size):
                copy.start()

    def drain():
        for group in range(count // size):
            for copy in stores(group):
                copy.wait()

    return wait, finish, drain


def late_kernel(coarse, x_ref, table_ref, taps_ref, out_ref, edge_ref, halo_ref, early_ref, *scratch):
    x_buf, out_buf, lines_a, lines_b, tail, x_sem, out_sem, early_sem = scratch
    lines = (lines_a, lines_b)
    beams, channels = out_ref.shape[:2]
    pair_rows = x_ref.shape[3] // (beams // 2)
    table = table_ref[...]
    coefficients = spread(taps_ref)

    def loads(s):
        where = x_ref.at[s, :, pl.ds(LATE * coarse, coarse)]
        return (pltpu.make_async_copy(where, x_buf.at[s], x_sem.at[s]),)

    def stores(s):
        own = pl.ds(s * coarse, coarse)
        rows = pl.ds(SPLIT, ROWS - SPLIT)
        return (pltpu.make_async_copy(out_buf.at[:, own], out_ref.at[:, own, rows], out_sem.at[s]),)

    wait, send, drain = grouped(channels, coarse, loads, stores)
    early = [
        pltpu.make_async_copy(x_ref.at[s, :, pl.ds(EARLY * coarse, coarse)], early_ref.at[s], early_sem.at[s])
        for s in range(x_ref.shape[0])
    ]
    for copy in early:
        copy.start()

    def make(c, slot, pair):
        rows = slice(pair * pair_rows, (pair + 1) * pair_rows)
        made = synth(x_buf[c // coarse, :, c % coarse, rows, :], table)
        for one in range(2):
            interleave(lines[slot], made, 2 * pair + 1 - one, one, 0)

    def use(c, slot, pair):
        for beam in (2 * pair, 2 * pair + 1):
            edge_ref[c, beam] = lines[slot][beam, : 2 * EDGE, :].astype(jnp.bfloat16)
            tail[2 * HALO * beam : 2 * HALO * (beam + 1), :] = lines[slot][beam, 2 * (HALF - HALO) : 2 * HALF, :]
            fir(lines[slot], beam, coefficients, 2 * EDGE, ROWS - SPLIT, out_buf, (beam, c))

    def finish(c):
        halo_ref[c] = tail[...].astype(jnp.bfloat16)
        send(c)

    in_turn(channels, beams // 2, wait, make, use, finish)
    drain()
    for copy in early:
        copy.wait()


def late(received, table, taps, coarse, beams):
    sources, blocks, _, rows, _ = received.shape
    channels = sources * coarse
    anywhere = pl.BlockSpec(memory_space=pl.ANY)
    inside = pl.BlockSpec(memory_space=pltpu.VMEM)
    edge = (channels, beams, 2 * EDGE, LANES)
    halo = (channels, beams * 2 * HALO, LANES)
    return pl.pallas_call(
        functools.partial(late_kernel, coarse),
        in_specs=[anywhere, inside, inside],
        out_specs=[anywhere, inside, inside, inside],
        out_shape=[
            jax.ShapeDtypeStruct((beams, channels, ROWS, LANES), jnp.bfloat16),
            jax.ShapeDtypeStruct(edge, jnp.bfloat16),
            jax.ShapeDtypeStruct(halo, jnp.bfloat16),
            jax.ShapeDtypeStruct((sources, blocks, coarse, rows, LANES), jnp.bfloat16),
        ],
        scratch_shapes=[
            pltpu.VMEM((sources, blocks, coarse, rows, LANES), jnp.bfloat16),
            pltpu.VMEM((beams, channels, ROWS - SPLIT, LANES), jnp.bfloat16),
            pltpu.VMEM((beams, 2 * HALF, LANES), jnp.float32),
            pltpu.VMEM((beams, 2 * HALF, LANES), jnp.float32),
            pltpu.VMEM((beams * 2 * HALO, LANES), jnp.float32),
            pltpu.SemaphoreType.DMA((sources,)),
            pltpu.SemaphoreType.DMA((sources,)),
            pltpu.SemaphoreType.DMA((sources,)),
        ],
        compiler_params=pltpu.CompilerParams(vmem_limit_bytes=VMEM),
        cost_estimate=pl.CostEstimate(
            flops=channels * beams * HALF * 2 * 256 * 256,
            bytes_accessed=2 * channels * beams * (4 * HALF + ROWS - SPLIT) * LANES,
            transcendentals=0,
        ),
        name="late",
    )(received, table, taps)


def middle_kernel(coarse, x_ref, edge_ref, table_ref, taps_ref, _, out_ref, begin_ref, *scratch):
    out_buf, lines_a, lines_b, out_sem = scratch
    lines = (lines_a, lines_b)
    beams, channels = out_ref.shape[:2]
    pair_rows = x_ref.shape[3] // (beams // 2)
    table = table_ref[...]
    coefficients = spread(taps_ref)

    def loads(s):
        return ()

    def stores(s):
        own = pl.ds(s * coarse, coarse)
        rows = pl.ds(HEAD, SPLIT - HEAD)
        return (pltpu.make_async_copy(out_buf.at[:, own], out_ref.at[:, own, rows], out_sem.at[s]),)

    wait, finish, drain = grouped(channels, coarse, loads, stores)

    def make(c, slot, pair):
        rows = slice(pair * pair_rows, (pair + 1) * pair_rows)
        made = synth(x_ref[c // coarse, :, c % coarse, rows, :], table)
        for one in range(2):
            beam = 2 * pair + one
            interleave(lines[slot], made, beam, one, 0)
            lines[slot][beam, 2 * HALF : SPLIT, :] = edge_ref[c, beam].astype(jnp.float32)

    def use(c, slot, pair):
        for beam in (2 * pair, 2 * pair + 1):
            begin_ref[c, beam] = lines[slot][beam, :HEAD, :].astype(jnp.bfloat16)
            fir(lines[slot], beam, coefficients, HEAD, SPLIT - HEAD, out_buf, (beam, c))

    in_turn(channels, beams // 2, wait, make, use, finish)
    drain()


def middle(early, edge, table, taps, out, coarse):
    sources = early.shape[0]
    beams, channels = out.shape[:2]
    anywhere = pl.BlockSpec(memory_space=pl.ANY)
    inside = pl.BlockSpec(memory_space=pltpu.VMEM)
    begin = (channels, beams, HEAD, LANES)
    return pl.pallas_call(
        functools.partial(middle_kernel, coarse),
        in_specs=[inside, inside, inside, inside, anywhere],
        out_specs=[anywhere, inside],
        out_shape=[jax.ShapeDtypeStruct(out.shape, out.dtype), jax.ShapeDtypeStruct(begin, jnp.bfloat16)],
        scratch_shapes=[
            pltpu.VMEM((beams, channels, SPLIT - HEAD, LANES), jnp.bfloat16),
            pltpu.VMEM((beams, SPLIT, LANES), jnp.float32),
            pltpu.VMEM((beams, SPLIT, LANES), jnp.float32),
            pltpu.SemaphoreType.DMA((sources,)),
        ],
        input_output_aliases={4: 0},
        compiler_params=pltpu.CompilerParams(vmem_limit_bytes=VMEM),
        cost_estimate=pl.CostEstimate(
            flops=channels * beams * HALF * 2 * 256 * 256,
            bytes_accessed=2 * channels * beams * (4 * HALF + SPLIT) * LANES,
            transcendentals=0,
        ),
        name="middle",
    )(early, edge, table, taps, out)


def first_kernel(begin_ref, halo_ref, taps_ref, _, out_ref, *scratch):
    out_buf, lines_a, lines_b, tail, out_sem = scratch
    lines = (lines_a, lines_b)
    beams, channels = out_ref.shape[:2]
    start = 32
    coefficients = spread(taps_ref)

    size = channels // 4

    def loads(s):
        return ()

    def stores(s):
        own = pl.ds(s * size, size)
        return (pltpu.make_async_copy(out_buf.at[:, own], out_ref.at[:, own, pl.ds(0, HEAD)], out_sem.at[s]),)

    wait, finish, drain = grouped(channels, size, loads, stores)

    def make(c, slot, pair):
        if pair == 0:
            tail[...] = halo_ref[c].astype(jnp.float32)
        for beam in (2 * pair, 2 * pair + 1):
            lines[slot][beam, start - 2 * HALO : start, :] = tail[2 * HALO * beam : 2 * HALO * (beam + 1), :]
            lines[slot][beam, start : start + HEAD, :] = begin_ref[c, beam].astype(jnp.float32)

    def use(c, slot, pair):
        for beam in (2 * pair, 2 * pair + 1):
            fir(lines[slot], beam, coefficients, start, HEAD, out_buf, (beam, c))

    in_turn(channels, beams // 2, wait, make, use, finish)
    drain()


def first(begin, halo, taps, out):
    beams, channels = out.shape[:2]
    anywhere = pl.BlockSpec(memory_space=pl.ANY)
    inside = pl.BlockSpec(memory_space=pltpu.VMEM)
    return pl.pallas_call(
        first_kernel,
        in_specs=[inside, inside, inside, anywhere],
        out_specs=anywhere,
        out_shape=jax.ShapeDtypeStruct(out.shape, out.dtype),
        scratch_shapes=[
            pltpu.VMEM((beams, channels, HEAD, LANES), jnp.bfloat16),
            pltpu.VMEM((beams, 32 + HEAD, LANES), jnp.float32),
            pltpu.VMEM((beams, 32 + HEAD, LANES), jnp.float32),
            pltpu.VMEM(halo.shape[1:], jnp.float32),
            pltpu.SemaphoreType.DMA((4,)),
        ],
        input_output_aliases={3: 0},
        compiler_params=pltpu.CompilerParams(vmem_limit_bytes=VMEM),
        cost_estimate=pl.CostEstimate(
            flops=channels * beams * HEAD * LANES * 24,
            bytes_accessed=2 * channels * beams * 3 * HEAD * LANES,
            transcendentals=0,
        ),
        name="first",
    )(begin, halo, taps, out)


def on_device(spectra, prototype):
    groups, blocks = lax.axis_size("beam"), lax.axis_size("tm")
    coarse, parts, fine, all_beams, _ = spectra.shape
    beams = all_beams // groups
    length = blocks * fine
    table = jnp.asarray(synth_table(length, blocks))
    packed = pack(spectra, UNITS, groups, blocks)
    moved = lax.all_to_all(packed, ("beam", "tm"), 0, 0, tiled=True)
    received = moved.reshape(groups, blocks, *moved.shape[1:])
    out, edge, halo, early = late(received, table, prototype, coarse, beams)
    halo = lax.ppermute(halo, "tm", [(i, i + 1) for i in range(blocks - 1)])
    out, begin = middle(early, edge, table, prototype, out, coarse)
    out = first(begin, halo, prototype, out)
    channels = groups * coarse
    out = out.reshape(beams, channels, 2 * HALF, 2, LANES).swapaxes(2, 3)
    return out.reshape(beams, channels, 2, 2 * HALF * LANES)


def solution(mesh):
    in_specs = (P("beam", None, "tm", None, None), P())
    out_specs = P("beam", None, None, "tm")
    return jax.shard_map(on_device, mesh=mesh, in_specs=in_specs, out_specs=out_specs, check_vma=False)
```

```python
import functools
import math

import jax
import jax.numpy as jnp
import numpy as np
from jax import lax
from jax.experimental import pallas as pl
from jax.experimental.pallas import tpu as pltpu
from jax.sharding import PartitionSpec as P

EARLY, LATE = 0, 1
UNITS = ((0, EARLY), (1, EARLY), (2, EARLY), (0, LATE), (1, LATE), (2, LATE))
LANES = 128
HALF = 64
EDGE = 16
HALO = 11
ROWS = 4 * HALF
SPLIT = 2 * (HALF + EDGE)
HEAD = 2 * EDGE
VMEM = 40 * 2**20


def synth_table(length, blocks):
    index = np.arange(length)
    angle = ((index[:, None] * index[None, :]) % length).astype(np.float32) * np.float32(2.0 * math.pi / length)
    cosine = np.cos(angle) / np.float32(math.sqrt(length))
    sine = np.sin(angle) / np.float32(math.sqrt(length))
    real_row = np.stack([cosine, sine], axis=1)
    imag_row = np.stack([-sine, cosine], axis=1)
    table = np.stack([real_row, imag_row], axis=0).reshape(2, blocks, length // blocks, 2 * length)
    return table.transpose(1, 0, 2, 3).reshape(2 * length, 2 * length).astype(jnp.bfloat16)


def pack_kernel(units, blocks, x_ref, y_ref, x_buf, y_buf, x_sem, y_sem):
    channels = sorted({c for c, _ in units})
    _, parts, fine, all_beams, frames = x_ref.shape
    beams = 16
    strips = all_beams // beams
    rows = y_ref.shape[2]

    def load(i, g):
        where = (slice(None), slice(None), pl.ds(pl.multiple_of(g * beams, beams), beams), slice(None))
        return pltpu.make_async_copy(x_ref.at[(channels[i], *where)], x_buf.at[(i, *where)], x_sem.at[i, g])

    def store(u, g):
        where = (pl.ds(g * 2 * blocks, 2 * blocks), u)
        return pltpu.make_async_copy(y_buf.at[where], y_ref.at[where], y_sem.at[u, g])

    for i in range(len(channels)):
        for g in range(strips):
            load(i, g).start()
    count = fine * beams
    row = lax.broadcasted_iota(jnp.int32, (count, count), 0)
    column = lax.broadcasted_iota(jnp.int32, (count, count), 1)
    pairs = beams // 4
    beam = row // (2 * pairs * fine) * (2 * pairs) + row // fine % pairs * 2 + row // (pairs * fine) % 2
    order = (column == row % fine * beams + beam).astype(jnp.bfloat16)
    lower = lax.broadcasted_iota(jnp.int32, (rows, LANES), 1) < HALF

    for i, channel in enumerate(channels):
        own = [(u, h) for u, (c, h) in enumerate(units) if c == channel]

        def strip(g, carry):
            load(i, g).wait()
            for t in range(0, blocks, 2):
                lines = x_buf[i, :, :, pl.ds(pl.multiple_of(g * beams, beams), beams), t * LANES : (t + 2) * LANES]
                moved = [
                    jnp.dot(order, lines[p].reshape(fine * beams, 2 * LANES), preferred_element_type=jnp.float32)
                    for p in range(parts)
                ]
                for part in range(2):
                    for group in range(2):
                        base = group * (rows)
                        lanes = slice(part * LANES, (part + 1) * LANES)
                        even, odd = [], []
                        for pair in range(rows // (parts * fine)):
                            for p in range(parts):
                                first = base + pair * fine
                                even.append(moved[p][first : first + fine, lanes])
                                first = base + rows // 2 + pair * fine
                                odd.append(moved[p][first : first + fine, lanes])
                        even = jnp.concatenate(even, axis=0)
                        odd = pltpu.roll(jnp.concatenate(odd, axis=0), HALF, 1)
                        for u, h in own:
                            made = jnp.where(lower, odd, even) if h == LATE else jnp.where(lower, even, odd)
                            y_buf[(2 * g + group) * blocks + t + part, u] = made.astype(jnp.bfloat16)
            for u, _ in own:
                store(u, g).start()
            return carry

        lax.fori_loop(0, strips, strip, 0)
    for u in range(len(units)):
        for g in range(strips):
            store(u, g).wait()


def pack(spectra, units, groups, blocks):
    coarse, parts, fine, beams, frames = spectra.shape
    rows = (beams // groups) // 2 * parts * fine
    strips = beams // 16
    channels = len({c for c, _ in units})
    shape = (groups * blocks, len(units), rows, LANES)
    return pl.pallas_call(
        functools.partial(pack_kernel, units, blocks),
        in_specs=[pl.BlockSpec(memory_space=pl.ANY)],
        out_specs=pl.BlockSpec(memory_space=pl.ANY),
        out_shape=jax.ShapeDtypeStruct(shape, jnp.bfloat16),
        scratch_shapes=[
            pltpu.VMEM((channels, parts, fine, beams, frames), jnp.bfloat16),
            pltpu.VMEM(shape, jnp.bfloat16),
            pltpu.SemaphoreType.DMA((channels, strips)),
            pltpu.SemaphoreType.DMA((len(units), strips)),
        ],
        compiler_params=pltpu.CompilerParams(vmem_limit_bytes=VMEM),
        cost_estimate=pl.CostEstimate(
            flops=channels * 2 * 256 * 256 * strips * frames,
            bytes_accessed=2 * channels * parts * fine * beams * frames + 2 * math.prod(shape),
            transcendentals=0,
        ),
        name="pack",
    )(spectra)


def synth(block, table):
    rows = block.shape[0] * block.shape[1]
    return lax.dot_general(
        block.reshape(rows, LANES), table, (((0,), (0,)), ((), ())), preferred_element_type=jnp.float32
    )


def interleave(lines_ref, made, beam, one, start):
    for q in range(2):
        lines_ref[beam, pl.ds(start + q, HALF, stride=2), :] = made[
            one * HALF : (one + 1) * HALF, q * LANES : (q + 1) * LANES
        ]


def fir(lines_ref, beam, coefficients, start, count, out_ref, where):
    window = {}
    done = []
    for m in range(count // 8):
        total = None
        for j, coefficient in enumerate(coefficients):
            key = (m - j // 4, j % 4)
            if key not in window:
                first = start + 8 * key[0] - 2 * key[1]
                window[key] = lines_ref[beam, first : first + 8, :]
            term = coefficient * window[key]
            total = term if total is None else total + term
        done.append(total)
        if len(done) == 2:
            out_ref[(*where, pl.ds(8 * (m - 1), 16), slice(None))] = jnp.concatenate(done, axis=0).astype(jnp.bfloat16)
            done = []


def spread(taps_ref):
    return [jnp.broadcast_to(taps_ref[j : j + 1, :], (8, LANES)) for j in range(taps_ref.shape[0])]


def in_turn(count, pairs, wait, make, use, finish):
    wait(0)
    for pair in range(pairs):
        make(0, 0, pair)

    def two(step, carry):
        for slot in range(2):
            now = 2 * step + slot
            if slot == 0:
                wait(now + 1)
                later = now + 1
            else:
                later = jnp.minimum(now + 1, count - 1)

                @pl.when(now + 1 < count)
                def _():
                    wait(later)

            for pair in range(pairs):
                make(later, 1 - slot, pair)
                use(now, slot, pair)
            finish(now)
        return carry

    lax.fori_loop(0, count // 2, two, 0)


def grouped(count, size, loads, stores):
    for group in range(count // size):
        for copy in loads(group):
            copy.start()

    def wait(i):
        @pl.when(i % size == 0)
        def _():
            for copy in loads(i // size):
                copy.wait()

    def finish(i):
        @pl.when(i % size == size - 1)
        def _():
            for copy in stores(i // size):
                copy.start()

    def drain():
        for group in range(count // size):
            for copy in stores(group):
                copy.wait()

    return wait, finish, drain


def late_kernel(coarse, x_ref, table_ref, taps_ref, out_ref, edge_ref, halo_ref, early_ref, *scratch):
    x_buf, out_buf, lines_a, lines_b, tail, x_sem, out_sem, early_sem = scratch
    lines = (lines_a, lines_b)
    beams, channels = out_ref.shape[:2]
    pair_rows = x_ref.shape[3] // (beams // 2)
    table = table_ref[...]
    coefficients = spread(taps_ref)

    def loads(s):
        where = x_ref.at[s, :, pl.ds(LATE * coarse, coarse)]
        return (pltpu.make_async_copy(where, x_buf.at[s], x_sem.at[s]),)

    def stores(s):
        own = pl.ds(s * coarse, coarse)
        rows = pl.ds(SPLIT, ROWS - SPLIT)
        return (pltpu.make_async_copy(out_buf.at[:, own], out_ref.at[:, own, rows], out_sem.at[s]),)

    wait, send, drain = grouped(channels, coarse, loads, stores)
    early = [
        pltpu.make_async_copy(x_ref.at[s, :, pl.ds(EARLY * coarse, coarse)], early_ref.at[s], early_sem.at[s])
        for s in range(x_ref.shape[0])
    ]
    for copy in early:
        copy.start()

    def make(c, slot, pair):
        rows = slice(pair * pair_rows, (pair + 1) * pair_rows)
        made = synth(x_buf[c // coarse, :, c % coarse, rows, :], table)
        for one in range(2):
            interleave(lines[slot], made, 2 * pair + 1 - one, one, 0)

    def use(c, slot, pair):
        for beam in (2 * pair, 2 * pair + 1):
            edge_ref[c, beam] = lines[slot][beam, : 2 * EDGE, :].astype(jnp.bfloat16)
            tail[2 * HALO * beam : 2 * HALO * (beam + 1), :] = lines[slot][beam, 2 * (HALF - HALO) : 2 * HALF, :]
            fir(lines[slot], beam, coefficients, 2 * EDGE, ROWS - SPLIT, out_buf, (beam, c))

    def finish(c):
        halo_ref[c] = tail[...].astype(jnp.bfloat16)
        send(c)

    in_turn(channels, beams // 2, wait, make, use, finish)
    drain()
    for copy in early:
        copy.wait()


def late(received, table, taps, coarse, beams):
    sources, blocks, _, rows, _ = received.shape
    channels = sources * coarse
    anywhere = pl.BlockSpec(memory_space=pl.ANY)
    inside = pl.BlockSpec(memory_space=pltpu.VMEM)
    edge = (channels, beams, 2 * EDGE, LANES)
    halo = (channels, beams * 2 * HALO, LANES)
    return pl.pallas_call(
        functools.partial(late_kernel, coarse),
        in_specs=[anywhere, inside, inside],
        out_specs=[anywhere, inside, inside, inside],
        out_shape=[
            jax.ShapeDtypeStruct((beams, channels, ROWS, LANES), jnp.bfloat16),
            jax.ShapeDtypeStruct(edge, jnp.bfloat16),
            jax.ShapeDtypeStruct(halo, jnp.bfloat16),
            jax.ShapeDtypeStruct((sources, blocks, coarse, rows, LANES), jnp.bfloat16),
        ],
        scratch_shapes=[
            pltpu.VMEM((sources, blocks, coarse, rows, LANES), jnp.bfloat16),
            pltpu.VMEM((beams, channels, ROWS - SPLIT, LANES), jnp.bfloat16),
            pltpu.VMEM((beams, 2 * HALF, LANES), jnp.float32),
            pltpu.VMEM((beams, 2 * HALF, LANES), jnp.float32),
            pltpu.VMEM((beams * 2 * HALO, LANES), jnp.float32),
            pltpu.SemaphoreType.DMA((sources,)),
            pltpu.SemaphoreType.DMA((sources,)),
            pltpu.SemaphoreType.DMA((sources,)),
        ],
        compiler_params=pltpu.CompilerParams(vmem_limit_bytes=VMEM),
        cost_estimate=pl.CostEstimate(
            flops=channels * beams * HALF * 2 * 256 * 256,
            bytes_accessed=2 * channels * beams * (4 * HALF + ROWS - SPLIT) * LANES,
            transcendentals=0,
        ),
        name="late",
    )(received, table, taps)


def middle_kernel(coarse, x_ref, edge_ref, table_ref, taps_ref, _, out_ref, begin_ref, *scratch):
    out_buf, lines_a, lines_b, out_sem = scratch
    lines = (lines_a, lines_b)
    beams, channels = out_ref.shape[:2]
    pair_rows = x_ref.shape[3] // (beams // 2)
    table = table_ref[...]
    coefficients = spread(taps_ref)

    def loads(s):
        return ()

    def stores(s):
        own = pl.ds(s * coarse, coarse)
        rows = pl.ds(HEAD, SPLIT - HEAD)
        return (pltpu.make_async_copy(out_buf.at[:, own], out_ref.at[:, own, rows], out_sem.at[s]),)

    wait, finish, drain = grouped(channels, coarse, loads, stores)

    def make(c, slot, pair):
        rows = slice(pair * pair_rows, (pair + 1) * pair_rows)
        made = synth(x_ref[c // coarse, :, c % coarse, rows, :], table)
        for one in range(2):
            beam = 2 * pair + one
            interleave(lines[slot], made, beam, one, 0)
            lines[slot][beam, 2 * HALF : SPLIT, :] = edge_ref[c, beam].astype(jnp.float32)

    def use(c, slot, pair):
        for beam in (2 * pair, 2 * pair + 1):
            begin_ref[c, beam] = lines[slot][beam, :HEAD, :].astype(jnp.bfloat16)
            fir(lines[slot], beam, coefficients, HEAD, SPLIT - HEAD, out_buf, (beam, c))

    in_turn(channels, beams // 2, wait, make, use, finish)
    drain()


def middle(early, edge, table, taps, out, coarse):
    sources = early.shape[0]
    beams, channels = out.shape[:2]
    anywhere = pl.BlockSpec(memory_space=pl.ANY)
    inside = pl.BlockSpec(memory_space=pltpu.VMEM)
    begin = (channels, beams, HEAD, LANES)
    return pl.pallas_call(
        functools.partial(middle_kernel, coarse),
        in_specs=[inside, inside, inside, inside, anywhere],
        out_specs=[anywhere, inside],
        out_shape=[jax.ShapeDtypeStruct(out.shape, out.dtype), jax.ShapeDtypeStruct(begin, jnp.bfloat16)],
        scratch_shapes=[
            pltpu.VMEM((beams, channels, SPLIT - HEAD, LANES), jnp.bfloat16),
            pltpu.VMEM((beams, SPLIT, LANES), jnp.float32),
            pltpu.VMEM((beams, SPLIT, LANES), jnp.float32),
            pltpu.SemaphoreType.DMA((sources,)),
        ],
        input_output_aliases={4: 0},
        compiler_params=pltpu.CompilerParams(vmem_limit_bytes=VMEM),
        cost_estimate=pl.CostEstimate(
            flops=channels * beams * HALF * 2 * 256 * 256,
            bytes_accessed=2 * channels * beams * (4 * HALF + SPLIT) * LANES,
            transcendentals=0,
        ),
        name="middle",
    )(early, edge, table, taps, out)


def first_kernel(begin_ref, halo_ref, taps_ref, _, out_ref, *scratch):
    out_buf, lines_a, lines_b, tail, out_sem = scratch
    lines = (lines_a, lines_b)
    beams, channels = out_ref.shape[:2]
    start = 32
    coefficients = spread(taps_ref)

    size = channels // 4

    def loads(s):
        return ()

    def stores(s):
        own = pl.ds(s * size, size)
        return (pltpu.make_async_copy(out_buf.at[:, own], out_ref.at[:, own, pl.ds(0, HEAD)], out_sem.at[s]),)

    wait, finish, drain = grouped(channels, size, loads, stores)

    def make(c, slot, pair):
        if pair == 0:
            tail[...] = halo_ref[c].astype(jnp.float32)
        for beam in (2 * pair, 2 * pair + 1):
            lines[slot][beam, start - 2 * HALO : start, :] = tail[2 * HALO * beam : 2 * HALO * (beam + 1), :]
            lines[slot][beam, start : start + HEAD, :] = begin_ref[c, beam].astype(jnp.float32)

    def use(c, slot, pair):
        for beam in (2 * pair, 2 * pair + 1):
            fir(lines[slot], beam, coefficients, start, HEAD, out_buf, (beam, c))

    in_turn(channels, beams // 2, wait, make, use, finish)
    drain()


def first(begin, halo, taps, out):
    beams, channels = out.shape[:2]
    anywhere = pl.BlockSpec(memory_space=pl.ANY)
    inside = pl.BlockSpec(memory_space=pltpu.VMEM)
    return pl.pallas_call(
        first_kernel,
        in_specs=[inside, inside, inside, anywhere],
        out_specs=anywhere,
        out_shape=jax.ShapeDtypeStruct(out.shape, out.dtype),
        scratch_shapes=[
            pltpu.VMEM((beams, channels, HEAD, LANES), jnp.bfloat16),
            pltpu.VMEM((beams, 32 + HEAD, LANES), jnp.float32),
            pltpu.VMEM((beams, 32 + HEAD, LANES), jnp.float32),
            pltpu.VMEM(halo.shape[1:], jnp.float32),
            pltpu.SemaphoreType.DMA((4,)),
        ],
        input_output_aliases={3: 0},
        compiler_params=pltpu.CompilerParams(vmem_limit_bytes=VMEM),
        cost_estimate=pl.CostEstimate(
            flops=channels * beams * HEAD * LANES * 24,
            bytes_accessed=2 * channels * beams * 3 * HEAD * LANES,
            transcendentals=0,
        ),
        name="first",
    )(begin, halo, taps, out)


def on_device(spectra, prototype):
    groups, blocks = lax.axis_size("beam"), lax.axis_size("tm")
    coarse, parts, fine, all_beams, _ = spectra.shape
    beams = all_beams // groups
    length = blocks * fine
    table = jnp.asarray(synth_table(length, blocks))
    packed = pack(spectra, UNITS, groups, blocks)
    moved = lax.all_to_all(packed, ("beam", "tm"), 0, 0, tiled=True)
    received = moved.reshape(groups, blocks, *moved.shape[1:])
    out, edge, halo, early = late(received, table, prototype, coarse, beams)
    halo = lax.ppermute(halo, "tm", [(i, i + 1) for i in range(blocks - 1)])
    out, begin = middle(early, edge, table, prototype, out, coarse)
    out = first(begin, halo, prototype, out)
    channels = groups * coarse
    out = out.reshape(beams, channels, 2 * HALF, 2, LANES).swapaxes(2, 3)
    return out.reshape(beams, channels, 2, 2 * HALF * LANES)


def solution(mesh):
    in_specs = (P("beam", None, "tm", None, None), P())
    out_specs = P("beam", None, None, "tm")
    return jax.shard_map(on_device, mesh=mesh, in_specs=in_specs, out_specs=out_specs, check_vma=False)
```

```python
import functools
import math

import jax
import jax.numpy as jnp
import numpy as np
from jax import lax
from jax.experimental import pallas as pl
from jax.experimental.pallas import tpu as pltpu
from jax.sharding import PartitionSpec as P

EARLY, LATE = 0, 1
UNITS = ((0, EARLY), (1, EARLY), (2, EARLY), (0, LATE), (1, LATE), (2, LATE))
LANES = 128
HALF = 64
EDGE = 24
HALO = 11
ROWS = 4 * HALF
SPLIT = 2 * (HALF + EDGE)
HEAD = 32
VMEM = 40 * 2**20


def synth_table(length, blocks):
    index = np.arange(length)
    angle = ((index[:, None] * index[None, :]) % length).astype(np.float32) * np.float32(2.0 * math.pi / length)
    cosine = np.cos(angle) / np.float32(math.sqrt(length))
    sine = np.sin(angle) / np.float32(math.sqrt(length))
    real_row = np.stack([cosine, sine], axis=1)
    imag_row = np.stack([-sine, cosine], axis=1)
    table = np.stack([real_row, imag_row], axis=0).reshape(2, blocks, length // blocks, 2 * length)
    return table.transpose(1, 0, 2, 3).reshape(2 * length, 2 * length).astype(jnp.bfloat16)


def pack_kernel(units, blocks, x_ref, y_ref, x_buf, y_buf, x_sem, y_sem):
    channels = sorted({c for c, _ in units})
    _, parts, fine, all_beams, frames = x_ref.shape
    beams = 16
    strips = all_beams // beams
    rows = y_ref.shape[2]

    def load(i, g):
        where = (slice(None), slice(None), pl.ds(pl.multiple_of(g * beams, beams), beams), slice(None))
        return pltpu.make_async_copy(x_ref.at[(channels[i], *where)], x_buf.at[(i, *where)], x_sem.at[i, g])

    def store(u, g):
        where = (pl.ds(g * 2 * blocks, 2 * blocks), u)
        return pltpu.make_async_copy(y_buf.at[where], y_ref.at[where], y_sem.at[u, g])

    for i in range(len(channels)):
        for g in range(strips):
            load(i, g).start()
    count = fine * beams
    row = lax.broadcasted_iota(jnp.int32, (count, count), 0)
    column = lax.broadcasted_iota(jnp.int32, (count, count), 1)
    pairs = beams // 4
    beam = row // (2 * pairs * fine) * (2 * pairs) + row // fine % pairs * 2 + row // (pairs * fine) % 2
    order = (column == row % fine * beams + beam).astype(jnp.bfloat16)
    lower = lax.broadcasted_iota(jnp.int32, (rows, LANES), 1) < HALF

    for i, channel in enumerate(channels):
        own = [(u, h) for u, (c, h) in enumerate(units) if c == channel]

        def strip(g, carry):
            load(i, g).wait()
            for t in range(0, blocks, 2):
                lines = x_buf[i, :, :, pl.ds(pl.multiple_of(g * beams, beams), beams), t * LANES : (t + 2) * LANES]
                moved = [
                    jnp.dot(order, lines[p].reshape(fine * beams, 2 * LANES), preferred_element_type=jnp.float32)
                    for p in range(parts)
                ]
                for part in range(2):
                    for group in range(2):
                        base = group * (rows)
                        lanes = slice(part * LANES, (part + 1) * LANES)
                        even, odd = [], []
                        for pair in range(rows // (parts * fine)):
                            for p in range(parts):
                                first = base + pair * fine
                                even.append(moved[p][first : first + fine, lanes])
                                first = base + rows // 2 + pair * fine
                                odd.append(moved[p][first : first + fine, lanes])
                        even = jnp.concatenate(even, axis=0)
                        odd = pltpu.roll(jnp.concatenate(odd, axis=0), HALF, 1)
                        for u, h in own:
                            made = jnp.where(lower, odd, even) if h == LATE else jnp.where(lower, even, odd)
                            y_buf[(2 * g + group) * blocks + t + part, u] = made.astype(jnp.bfloat16)
            for u, _ in own:
                store(u, g).start()
            return carry

        lax.fori_loop(0, strips, strip, 0)
    for u in range(len(units)):
        for g in range(strips):
            store(u, g).wait()


def pack(spectra, units, groups, blocks):
    coarse, parts, fine, beams, frames = spectra.shape
    rows = (beams // groups) // 2 * parts * fine
    strips = beams // 16
    channels = len({c for c, _ in units})
    shape = (groups * blocks, len(units), rows, LANES)
    return pl.pallas_call(
        functools.partial(pack_kernel, units, blocks),
        in_specs=[pl.BlockSpec(memory_space=pl.ANY)],
        out_specs=pl.BlockSpec(memory_space=pl.ANY),
        out_shape=jax.ShapeDtypeStruct(shape, jnp.bfloat16),
        scratch_shapes=[
            pltpu.VMEM((channels, parts, fine, beams, frames), jnp.bfloat16),
            pltpu.VMEM(shape, jnp.bfloat16),
            pltpu.SemaphoreType.DMA((channels, strips)),
            pltpu.SemaphoreType.DMA((len(units), strips)),
        ],
        compiler_params=pltpu.CompilerParams(vmem_limit_bytes=VMEM),
        cost_estimate=pl.CostEstimate(
            flops=channels * 2 * 256 * 256 * strips * frames,
            bytes_accessed=2 * channels * parts * fine * beams * frames + 2 * math.prod(shape),
            transcendentals=0,
        ),
        name="pack",
    )(spectra)


def synth(block, table):
    rows = block.shape[0] * block.shape[1]
    made = lax.dot_general(
        block.reshape(rows, LANES), table, (((0,), (0,)), ((), ())), preferred_element_type=jnp.float32
    )
    return made.astype(jnp.bfloat16).astype(jnp.float32)


def interleave(lines_ref, made, beam, one, start):
    for q in range(2):
        lines_ref[beam, pl.ds(start + q, HALF, stride=2), :] = made[
            one * HALF : (one + 1) * HALF, q * LANES : (q + 1) * LANES
        ]


def fir(lines_ref, beam, coefficients, start, count, out_ref, where):
    window = {}
    done = []
    for m in range(count // 8):
        total = None
        for j, coefficient in enumerate(coefficients):
            key = (m - j // 4, j % 4)
            if key not in window:
                first = start + 8 * key[0] - 2 * key[1]
                window[key] = lines_ref[beam, first : first + 8, :]
            term = coefficient * window[key]
            total = term if total is None else total + term
        done.append(total)
        if len(done) == 2:
            out_ref[(*where, pl.ds(8 * (m - 1), 16), slice(None))] = jnp.concatenate(done, axis=0).astype(jnp.bfloat16)
            done = []


def spread(taps_ref):
    return [jnp.broadcast_to(taps_ref[j : j + 1, :], (8, LANES)) for j in range(taps_ref.shape[0])]


def in_turn(count, pairs, wait, make, use, finish):
    wait(0)
    for pair in range(pairs):
        make(0, 0, pair)

    def two(step, carry):
        for slot in range(2):
            now = 2 * step + slot
            if slot == 0:
                wait(now + 1)
                later = now + 1
            else:
                later = jnp.minimum(now + 1, count - 1)

                @pl.when(now + 1 < count)
                def _():
                    wait(later)

            for pair in range(pairs):
                make(later, 1 - slot, pair)
                use(now, slot, pair)
            finish(now)
        return carry

    lax.fori_loop(0, count // 2, two, 0)


def grouped(count, size, loads, stores):
    for group in range(count // size):
        for copy in loads(group):
            copy.start()

    def wait(i):
        @pl.when(i % size == 0)
        def _():
            for copy in loads(i // size):
                copy.wait()

    def finish(i):
        @pl.when(i % size == size - 1)
        def _():
            for copy in stores(i // size):
                copy.start()

    def drain():
        for group in range(count // size):
            for copy in stores(group):
                copy.wait()

    return wait, finish, drain


def late_kernel(coarse, x_ref, table_ref, taps_ref, out_ref, edge_ref, halo_ref, early_ref, *scratch):
    x_buf, out_buf, lines_a, lines_b, tail, x_sem, out_sem, early_sem = scratch
    lines = (lines_a, lines_b)
    beams, channels = out_ref.shape[:2]
    pair_rows = x_ref.shape[3] // (beams // 2)
    table = table_ref[...]
    coefficients = spread(taps_ref)

    def loads(s):
        where = x_ref.at[s, :, pl.ds(LATE * coarse, coarse)]
        return (pltpu.make_async_copy(where, x_buf.at[s], x_sem.at[s]),)

    def stores(s):
        own = pl.ds(s * coarse, coarse)
        rows = pl.ds(SPLIT, ROWS - SPLIT)
        return (pltpu.make_async_copy(out_buf.at[:, own], out_ref.at[:, own, rows], out_sem.at[s]),)

    wait, send, drain = grouped(channels, coarse, loads, stores)
    early = [
        pltpu.make_async_copy(x_ref.at[s, :, pl.ds(EARLY * coarse, coarse)], early_ref.at[s], early_sem.at[s])
        for s in range(x_ref.shape[0])
    ]
    for copy in early:
        copy.start()

    def make(c, slot, pair):
        rows = slice(pair * pair_rows, (pair + 1) * pair_rows)
        made = synth(x_buf[c // coarse, :, c % coarse, rows, :], table)
        for one in range(2):
            interleave(lines[slot], made, 2 * pair + 1 - one, one, 0)

    def use(c, slot, pair):
        for beam in (2 * pair, 2 * pair + 1):
            edge_ref[c, beam] = lines[slot][beam, : 2 * EDGE, :].astype(jnp.bfloat16)
            tail[2 * HALO * beam : 2 * HALO * (beam + 1), :] = lines[slot][beam, 2 * (HALF - HALO) : 2 * HALF, :]
            fir(lines[slot], beam, coefficients, 2 * EDGE, ROWS - SPLIT, out_buf, (beam, c))

    def finish(c):
        halo_ref[c] = tail[...].astype(jnp.bfloat16)
        send(c)

    in_turn(channels, beams // 2, wait, make, use, finish)
    drain()
    for copy in early:
        copy.wait()


def late(received, table, taps, coarse, beams):
    sources, blocks, _, rows, _ = received.shape
    channels = sources * coarse
    anywhere = pl.BlockSpec(memory_space=pl.ANY)
    inside = pl.BlockSpec(memory_space=pltpu.VMEM)
    edge = (channels, beams, 2 * EDGE, LANES)
    halo = (channels, beams * 2 * HALO, LANES)
    return pl.pallas_call(
        functools.partial(late_kernel, coarse),
        in_specs=[anywhere, inside, inside],
        out_specs=[anywhere, inside, inside, inside],
        out_shape=[
            jax.ShapeDtypeStruct((beams, channels, ROWS, LANES), jnp.bfloat16),
            jax.ShapeDtypeStruct(edge, jnp.bfloat16),
            jax.ShapeDtypeStruct(halo, jnp.bfloat16),
            jax.ShapeDtypeStruct((sources, blocks, coarse, rows, LANES), jnp.bfloat16),
        ],
        scratch_shapes=[
            pltpu.VMEM((sources, blocks, coarse, rows, LANES), jnp.bfloat16),
            pltpu.VMEM((beams, channels, ROWS - SPLIT, LANES), jnp.bfloat16),
            pltpu.VMEM((beams, 2 * HALF, LANES), jnp.float32),
            pltpu.VMEM((beams, 2 * HALF, LANES), jnp.float32),
            pltpu.VMEM((beams * 2 * HALO, LANES), jnp.float32),
            pltpu.SemaphoreType.DMA((sources,)),
            pltpu.SemaphoreType.DMA((sources,)),
            pltpu.SemaphoreType.DMA((sources,)),
        ],
        compiler_params=pltpu.CompilerParams(vmem_limit_bytes=VMEM),
        cost_estimate=pl.CostEstimate(
            flops=channels * beams * HALF * 2 * 256 * 256,
            bytes_accessed=2 * channels * beams * (4 * HALF + ROWS - SPLIT) * LANES,
            transcendentals=0,
        ),
        name="late",
    )(received, table, taps)


def middle_kernel(coarse, x_ref, edge_ref, table_ref, taps_ref, _, out_ref, begin_ref, *scratch):
    out_buf, lines_a, lines_b, out_sem = scratch
    lines = (lines_a, lines_b)
    beams, channels = out_ref.shape[:2]
    pair_rows = x_ref.shape[3] // (beams // 2)
    table = table_ref[...]
    coefficients = spread(taps_ref)

    def loads(s):
        return ()

    def stores(s):
        own = pl.ds(s * coarse, coarse)
        rows = pl.ds(HEAD, SPLIT - HEAD)
        return (pltpu.make_async_copy(out_buf.at[:, own], out_ref.at[:, own, rows], out_sem.at[s]),)

    wait, finish, drain = grouped(channels, coarse, loads, stores)

    def make(c, slot, pair):
        rows = slice(pair * pair_rows, (pair + 1) * pair_rows)
        made = synth(x_ref[c // coarse, :, c % coarse, rows, :], table)
        for one in range(2):
            beam = 2 * pair + one
            interleave(lines[slot], made, beam, one, 0)
            lines[slot][beam, 2 * HALF : SPLIT, :] = edge_ref[c, beam].astype(jnp.float32)

    def use(c, slot, pair):
        for beam in (2 * pair, 2 * pair + 1):
            begin_ref[c, beam] = lines[slot][beam, :HEAD, :].astype(jnp.bfloat16)
            fir(lines[slot], beam, coefficients, HEAD, SPLIT - HEAD, out_buf, (beam, c))

    in_turn(channels, beams // 2, wait, make, use, finish)
    drain()


def middle(early, edge, table, taps, out, coarse):
    sources = early.shape[0]
    beams, channels = out.shape[:2]
    anywhere = pl.BlockSpec(memory_space=pl.ANY)
    inside = pl.BlockSpec(memory_space=pltpu.VMEM)
    begin = (channels, beams, HEAD, LANES)
    return pl.pallas_call(
        functools.partial(middle_kernel, coarse),
        in_specs=[inside, inside, inside, inside, anywhere],
        out_specs=[anywhere, inside],
        out_shape=[jax.ShapeDtypeStruct(out.shape, out.dtype), jax.ShapeDtypeStruct(begin, jnp.bfloat16)],
        scratch_shapes=[
            pltpu.VMEM((beams, channels, SPLIT - HEAD, LANES), jnp.bfloat16),
            pltpu.VMEM((beams, SPLIT, LANES), jnp.float32),
            pltpu.VMEM((beams, SPLIT, LANES), jnp.float32),
            pltpu.SemaphoreType.DMA((sources,)),
        ],
        input_output_aliases={4: 0},
        compiler_params=pltpu.CompilerParams(vmem_limit_bytes=VMEM),
        cost_estimate=pl.CostEstimate(
            flops=channels * beams * HALF * 2 * 256 * 256,
            bytes_accessed=2 * channels * beams * (4 * HALF + SPLIT) * LANES,
            transcendentals=0,
        ),
        name="middle",
    )(early, edge, table, taps, out)


def first_kernel(begin_ref, halo_ref, taps_ref, _, out_ref, *scratch):
    out_buf, lines_a, lines_b, tail, out_sem = scratch
    lines = (lines_a, lines_b)
    beams, channels = out_ref.shape[:2]
    start = 32
    coefficients = spread(taps_ref)

    size = channels // 4

    def loads(s):
        return ()

    def stores(s):
        own = pl.ds(s * size, size)
        return (pltpu.make_async_copy(out_buf.at[:, own], out_ref.at[:, own, pl.ds(0, HEAD)], out_sem.at[s]),)

    wait, finish, drain = grouped(channels, size, loads, stores)

    def make(c, slot, pair):
        if pair == 0:
            tail[...] = halo_ref[c].astype(jnp.float32)
        for beam in (2 * pair, 2 * pair + 1):
            lines[slot][beam, start - 2 * HALO : start, :] = tail[2 * HALO * beam : 2 * HALO * (beam + 1), :]
            lines[slot][beam, start : start + HEAD, :] = begin_ref[c, beam].astype(jnp.float32)

    def use(c, slot, pair):
        for beam in (2 * pair, 2 * pair + 1):
            fir(lines[slot], beam, coefficients, start, HEAD, out_buf, (beam, c))

    in_turn(channels, beams // 2, wait, make, use, finish)
    drain()


def first(begin, halo, taps, out):
    beams, channels = out.shape[:2]
    anywhere = pl.BlockSpec(memory_space=pl.ANY)
    inside = pl.BlockSpec(memory_space=pltpu.VMEM)
    return pl.pallas_call(
        first_kernel,
        in_specs=[inside, inside, inside, anywhere],
        out_specs=anywhere,
        out_shape=jax.ShapeDtypeStruct(out.shape, out.dtype),
        scratch_shapes=[
            pltpu.VMEM((beams, channels, HEAD, LANES), jnp.bfloat16),
            pltpu.VMEM((beams, 32 + HEAD, LANES), jnp.float32),
            pltpu.VMEM((beams, 32 + HEAD, LANES), jnp.float32),
            pltpu.VMEM(halo.shape[1:], jnp.float32),
            pltpu.SemaphoreType.DMA((4,)),
        ],
        input_output_aliases={3: 0},
        compiler_params=pltpu.CompilerParams(vmem_limit_bytes=VMEM),
        cost_estimate=pl.CostEstimate(
            flops=channels * beams * HEAD * LANES * 24,
            bytes_accessed=2 * channels * beams * 3 * HEAD * LANES,
            transcendentals=0,
        ),
        name="first",
    )(begin, halo, taps, out)


def on_device(spectra, prototype):
    groups, blocks = lax.axis_size("beam"), lax.axis_size("tm")
    coarse, parts, fine, all_beams, _ = spectra.shape
    beams = all_beams // groups
    length = blocks * fine
    table = jnp.asarray(synth_table(length, blocks))
    packed = pack(spectra, UNITS, groups, blocks)
    moved = lax.all_to_all(packed, ("beam", "tm"), 0, 0, tiled=True)
    received = moved.reshape(groups, blocks, *moved.shape[1:])
    out, edge, halo, early = late(received, table, prototype, coarse, beams)
    halo = lax.ppermute(halo, "tm", [(i, i + 1) for i in range(blocks - 1)])
    out, begin = middle(early, edge, table, prototype, out, coarse)
    out = first(begin, halo, prototype, out)
    channels = groups * coarse
    out = out.reshape(beams, channels, 2 * HALF, 2, LANES).swapaxes(2, 3)
    return out.reshape(beams, channels, 2, 2 * HALF * LANES)


def solution(mesh):
    in_specs = (P("beam", None, "tm", None, None), P())
    out_specs = P("beam", None, None, "tm")
    return jax.shard_map(on_device, mesh=mesh, in_specs=in_specs, out_specs=out_specs, check_vma=False)
```
